256 devices in a mesh: dp: 32 (over y, z_lo, core), pos: 8 (over z_hi, x).
Axes of the slice: x: 4, y: 4, z: 8 (z_hi: 2, z_lo: 4; z = z_hi * 4 + z_lo), core: 2. Of those that a mesh axis runs over, the one named last changes fastest.
Arguments:
- inputs: bfloat16 [64, 2048, 512], P('dp', 'pos'), may hold values from -6 to 6
- pre_act: bfloat16 [64, 2048, 512], P('dp', 'pos'), may hold values from -6 to 6
- grad_out: bfloat16 [64, 2048, 512], P('dp', 'pos'), may hold values from -6 to 6
- weight: bfloat16 [512, 9, 512], P(('dp', 'pos')), may hold values from -0.09375 to 0.09375
Outputs:
- grad_input: bfloat16 [64, 2048, 512], P('dp', 'pos')
- grad_weight: float32 [512, 9, 512], P(('dp', 'pos'))
The draws below stay inside these ranges and needn't reach their ends.
All inputs are finite; a program needn't handle non-finite values.
Results may differ from the reference program's by a relative error of at most 0.005.
Values may be sent and summed in bfloat16 or wider, within the bound.
A program may use at most 128 MiB of HBM per device.

```python
import jax
import jax.numpy as jnp
from jax import lax

C = 512
K = 9
SEQS = 64
L = 2048


def raised(array, rng, source, target, blocks, factor):
    def block_of(dim):
        return (jnp.arange(array.shape[dim]) // (array.shape[dim] // blocks)).reshape((-1,) + (1,) * (array.ndim - 1 - dim))

    one_side = jax.random.permutation(rng, blocks)[block_of(target)]
    second = (block_of(target) + blocks // 2) % blocks
    return jnp.where((block_of(source) == one_side) | (block_of(source) == second), factor * array, array)


def levels(stream_key, extent, pieces, least, top_value):
    level = 1.0
    for axis_at, blocks in pieces:
        draws = jax.random.uniform(jax.random.fold_in(jax.random.fold_in(stream_key, 6), axis_at), (blocks,), jnp.float32, least / len(pieces), top_value / len(pieces))
        level = level * jnp.repeat(jnp.exp(draws), extent[axis_at] // blocks).reshape((-1,) + (1,) * (len(extent) - 1 - axis_at))
    return level


def normal_values(key, dims, width, limit, cuts=(), dtype=jnp.bfloat16):
    gain = levels(key, dims, cuts, -0.22, 0.18) if cuts else 1.0
    result = jax.random.normal(key, dims, jnp.float32) * width * gain
    return jnp.minimum(jnp.maximum(result, -limit), limit).astype(dtype)


def heavy_noise(rng, dims, deviation, limit, cuts, heavy, held_as=jnp.bfloat16):
    array = deviation * jax.random.normal(rng, dims, jnp.float32)
    if cuts:
        array = array * levels(rng, dims, cuts, -0.22, 0.18)
    return jnp.clip(raised(array, jax.random.fold_in(rng, 3), *heavy), -limit, limit).astype(held_as)


def setup_inputs(seed: int = 0) -> dict:
    keys = jax.random.split(jax.random.key(seed), 5)
    return {
        "inputs": heavy_noise(keys[0], (SEQS, L, C), 1.0, 6.0, ((0, 32), (1, 8)), (1, 2, 8, 2.0)),
        "pre_act": normal_values(keys[1], (SEQS, L, C), 1.0, 6.0, ((0, 32), (1, 8))),
        "grad_out": normal_values(keys[2], (SEQS, L, C), 1.0, 6.0, ((0, 32), (1, 8))),
        "weight": normal_values(keys[3], (C, K, C), (K * C) ** -0.5, 0.09375, ((0, 256),)),
    }


def gelu_slope(values):
    cdf = 0.5 * (1.0 + lax.erf(values * 0.7071067811865476))
    return cdf + values * jnp.exp(-0.5 * values * values) * 0.3989422804014327


def transpose_conv(grad_pre, weight):
    half_width = (K - 1) // 2
    padded = jnp.pad(grad_pre, ((half_width, half_width), (0, 0)))
    total = jnp.zeros((L, C), jnp.float32)
    for offset in range(K):
        begin = K - 1 - offset
        total = total + jnp.dot(padded[begin:begin + L], weight[:, offset, :].T, preferred_element_type=jnp.float32)
    return total


def weight_terms(values, grad_pre):
    half_width = (K - 1) // 2
    padded = jnp.pad(values, ((half_width, half_width), (0, 0)))
    return jnp.stack([jnp.dot(padded[offset:offset + L].T, grad_pre, preferred_element_type=jnp.float32) for offset in range(K)], axis=1)


def reference(inputs, pre_act, grad_out, weight):
    def per_sequence(carry, sequence):
        x_seq, pre_seq, out_seq = sequence
        grad_pre = (out_seq.astype(jnp.float32) * gelu_slope(pre_seq.astype(jnp.float32))).astype(jnp.bfloat16)
        rev_in = x_seq[::-1, ::-1]
        rev_grad = grad_pre[::-1, ::-1]
        grad_in = transpose_conv(grad_pre, weight) + transpose_conv(rev_grad, weight)[::-1, ::-1]
        carry = carry + weight_terms(x_seq, grad_pre) + weight_terms(rev_in, rev_grad)
        return carry, grad_in.astype(jnp.bfloat16)

    total, grad_input = lax.scan(per_sequence, jnp.zeros((C, K, C), jnp.float32), (inputs, pre_act, grad_out))
    return grad_input, total
```

```python
import jax
import jax.numpy as jnp
import numpy as np
from jax import lax
from jax.experimental import pallas as pl
from jax.experimental.pallas import tpu as pltpu
from jax.sharding import PartitionSpec as P

K = 9
HALO = 8
GROUPS = 3
TAPS = K // GROUPS
MESH = pl.DeviceIdType.MESH
F32 = jnp.float32
BF16 = jnp.bfloat16


def gelu_slope(values):
    cdf = 0.5 * (1.0 + lax.erf(values * 0.7071067811865476))
    return cdf + values * jnp.exp(-0.5 * values * values) * 0.3989422804014327


def device(x, y, z, c):
    return ((y * 4 + z % 4) * 2 + c, (z // 4) * 4 + x)


def channel_orders():
    sorts = np.zeros((2, 512, 512), np.float32)
    for core in range(2):
        for q in range(4):
            for p in range(4):
                x, y = (p, q) if core == 0 else (q, p)
                for z in range(8):
                    for c in range(2):
                        row = (q * 4 + p) * 16 + 2 * z + c
                        dp, pos = device(x, y, z, c)
                        even = 2 * (dp * 8 + pos)
                        sorts[core, row, even] = 1.0
                        sorts[core, 256 + row, 511 - even] = 1.0
    return sorts.astype(jnp.bfloat16)


def dot(a, b, ca, cb):
    return lax.dot_general(a, b, (((ca,), (cb,)), ((), ())), preferred_element_type=F32)


def kernel(
    w_ref, pre_hbm, go_hbm, x_hbm, sort_hbm, gi_hbm, gw_hbm,
    pv, gv, xv, sv, gp, gfp, xt, rk, edge_out, edge_in,
    mirror_out, mirror_in, zb, wb_own, wb_oth,
    sf, sd, dr, qs, qr, t1, ps, pr, zs, zr, fs, fr, ow, acc, eo, gi,
    load_sem, store_sem, m_s, m_r, h_s, h_r, z_s, z_r, p_s, p_r, q_s, q_r, d_s, d_r,
    rd_s, rd_r, rq_s, rq_r, rp_s, rp_r, rz_s, rz_r, f_s, f_r,
):
    dp, pos = lax.axis_index("dp"), lax.axis_index("pos")
    y, c = dp // 8, dp % 2
    x = pos % 4
    z = (pos // 4) * 4 + (dp // 2) % 4
    p = x * (1 - c) + y * c
    q = y * (1 - c) + x * c
    z_peers = [device(x, y, (z + i) % 8, c) for i in range(1, 8)]
    p_peers = [device((x + i * (1 - c)) % 4, (y + i * c) % 4, z, c) for i in range(1, 4)]
    q_peers = [device((x + i * c) % 4, (y + i * (1 - c)) % 4, z, c) for i in range(1, 4)]
    twin = device(x, y, z, 1 - c)
    mirror_a = device(3 - x, 3 - y, 7 - z, 1 - c)
    mirror_b = device(3 - x, 3 - y, 7 - z, c)
    after, before = (dp, (pos + 1) % 8), (dp, (pos + 7) % 8)

    barrier = pltpu.get_barrier_semaphore()
    peers = z_peers + p_peers + q_peers + [twin, mirror_a, mirror_b, after, before]
    for peer in peers:
        pl.semaphore_signal(barrier, inc=1, device_id=peer, device_id_type=MESH)

    own_lanes = pl.ds(pl.multiple_of(c * 256, 256), 256)
    oth_lanes = pl.ds(pl.multiple_of((1 - c) * 256, 256), 256)
    loads = [
        pltpu.make_async_copy(pre_hbm.at[:, :, own_lanes], pv.at[0], load_sem.at[0]),
        pltpu.make_async_copy(go_hbm.at[:, :, own_lanes], gv.at[0], load_sem.at[1]),
        pltpu.make_async_copy(pre_hbm.at[:, :, oth_lanes], pv.at[1], load_sem.at[2]),
        pltpu.make_async_copy(go_hbm.at[:, :, oth_lanes], gv.at[1], load_sem.at[3]),
        pltpu.make_async_copy(x_hbm, xv, load_sem.at[4]),
        pltpu.make_async_copy(sort_hbm.at[c], sv, load_sem.at[5]),
    ]
    for load in loads:
        load.start()

    sends = []

    def send(src, dst, send_sem, recv_sem, peer):
        copy = pltpu.make_async_remote_copy(
            src_ref=src, dst_ref=dst, send_sem=send_sem, recv_sem=recv_sem,
            device_id=peer, device_id_type=MESH,
        )
        copy.start()
        sends.append(copy)
        return copy

    rows_i = lax.broadcasted_iota(jnp.int32, (256, 256), 0)
    cols_i = lax.broadcasted_iota(jnp.int32, (256, 256), 1)
    flip = jnp.where(rows_i + cols_i == 255, 1.0, 0.0).astype(BF16)

    w0_own = w_ref[0, :, own_lanes].astype(F32)
    mirror_out[0] = w_ref[1, :, own_lanes].astype(F32)
    mirror_out[1] = w_ref[1, :, oth_lanes].astype(F32)
    mirror_out[2] = w_ref[0, :, oth_lanes].astype(F32)

    zeros = jnp.zeros((2, HALO, 512), F32)
    for padded in (gp, gfp):
        padded[:, 0:HALO, :] = zeros
        padded[:, HALO + 256 : 2 * HALO + 256, :] = zeros
    for half in range(2):
        loads[2 * half].wait()
        loads[2 * half + 1].wait()
        for seq in range(2):

            def slope(i, carry, half=half, seq=seq):
                rows = pl.ds(pl.multiple_of(i * 32, 32), 32)
                values = pv[half, seq, rows, :].astype(F32)
                grad = gv[half, seq, rows, :].astype(F32) * gelu_slope(values)
                place = pl.ds(pl.multiple_of(HALO + i * 32, 8), 32)
                gp[seq, place, half * 256 : half * 256 + 256] = grad.astype(BF16).astype(F32)
                return carry

            lax.fori_loop(0, 8, slope, 0)
    edge_out[0] = gp[:, 256 : 256 + HALO, :]
    edge_out[1] = gp[:, HALO : 2 * HALO, :]

    pl.semaphore_wait(barrier, len(peers))
    mirror = [
        send(mirror_out.at[i], mirror_in.at[i], m_s.at[i], m_r.at[i], peer)
        for i, peer in enumerate((mirror_a, mirror_b, twin))
    ]
    edges = [
        send(edge_out.at[i], edge_in.at[i], h_s.at[i], h_r.at[i], peer)
        for i, peer in enumerate((after, before))
    ]

    for seq in range(2):
        main = gp[seq, HALO : HALO + 256, :].astype(BF16)
        gfp[seq, HALO : HALO + 256, 0:256] = dot(main[:, 256:512], flip, 1, 0)
        gfp[seq, HALO : HALO + 256, 256:512] = dot(main[:, 0:256], flip, 1, 0)
    loads[4].wait()
    loads[5].wait()
    for seq in range(2):
        sorted_x = dot(sv[...], xv[seq], 1, 1).astype(BF16)
        xt[:, seq * 256 : seq * 256 + 256] = sorted_x[0:256]
        xt[:, 512 + seq * 256 : 768 + seq * 256] = sorted_x[256:512]
    for k in range(K):
        for seq in range(2):
            rk[k, seq * 256 : seq * 256 + 256, :] = gp[seq, 12 - k : 268 - k, :].astype(BF16)
            rk[k, 512 + seq * 256 : 768 + seq * 256, :] = gfp[seq, 4 + k : 260 + k, :].astype(BF16)

    for copy in mirror:
        copy.wait_recv()
    rev_a = dot(mirror_in[0].astype(BF16), flip, 1, 0)
    rev_b = dot(mirror_in[1].astype(BF16), flip, 1, 0)
    w0_oth = mirror_in[2]
    for k in range(K):
        zb[k, pl.ds(2 * z + c, 1), :] = w0_own[k : k + 1] + rev_a[8 - k : 9 - k]
        zb[k, pl.ds(2 * z + 1 - c, 1), :] = w0_oth[k : k + 1] + rev_b[8 - k : 9 - k]
    mine = pl.ds(2 * z, 2)
    z_gather = [
        send(zb.at[:, mine, :], zb.at[:, mine, :], z_s.at[i], z_r.at[i], peer)
        for i, peer in enumerate(z_peers)
    ]

    for copy in edges:
        copy.wait_recv()
    low = jnp.where(pos == 0, 0.0, edge_in[0])
    high = jnp.where(pos == 7, 0.0, edge_in[1])
    gp[:, 0:HALO, :] = low
    gp[:, HALO + 256 : 2 * HALO + 256, :] = high
    both = jnp.concatenate([low[0], low[1], high[0], high[1]], axis=0).astype(BF16)
    both = jnp.concatenate(
        [dot(both[:, 256:512], flip, 1, 0), dot(both[:, 0:256], flip, 1, 0)], axis=1
    )
    for seq in range(2):
        gfp[seq, 0:HALO, :] = both[seq * HALO : seq * HALO + HALO]
        gfp[seq, HALO + 256 : 2 * HALO + 256, :] = both[(2 + seq) * HALO : (3 + seq) * HALO]
    for k in range(K):
        for seq in range(2):
            for start in (0, 240):
                rk[k, seq * 256 + start : seq * 256 + start + 16, :] = gp[
                    seq, 12 - k + start : 28 - k + start, :
                ].astype(BF16)
                rk[k, 512 + seq * 256 + start : 528 + seq * 256 + start, :] = gfp[
                    seq, 4 + k + start : 20 + k + start, :
                ].astype(BF16)

    def products(group):
        def one(k, carry):
            terms = dot(xt[...], rk[k], 1, 0)
            for a in range(4):
                for b in range(4):
                    rows = slice((a * 4 + b) * 16, (a * 4 + b) * 16 + 16)
                    sf[k, a, b] = terms[rows, 0:256]
                    sd[k, b, a] = terms[rows, 256:512].astype(BF16)
            return carry

        lax.fori_loop(group * TAPS, group * TAPS + TAPS, one, 0)
        taps = pl.ds(group * TAPS, TAPS)
        return send(sd.at[taps], dr.at[taps], rd_s.at[group], rd_r.at[group], twin)

    def chip_sum(group, copy):
        copy.wait_recv()

        def one(k, carry):
            total = sf[k] + dr[k].astype(F32)
            sf[k] = total
            qs[k] = total.astype(BF16)
            return carry

        lax.fori_loop(group * TAPS, group * TAPS + TAPS, one, 0)
        taps = pl.ds(group * TAPS, TAPS)
        return [
            send(
                qs.at[taps, (q + i) % 4], qr.at[i - 1, taps],
                rq_s.at[group, i - 1], rq_r.at[group, i - 1], q_peers[i - 1],
            )
            for i in range(1, 4)
        ]

    def q_sum(group, copies):
        for copy in copies:
            copy.wait_recv()

        def one(k, carry):
            total = sf[k, q] + qr[0, k].astype(F32) + qr[1, k].astype(F32) + qr[2, k].astype(F32)
            t1[k] = total
            ps[k] = total.astype(BF16)
            return carry

        lax.fori_loop(group * TAPS, group * TAPS + TAPS, one, 0)
        taps = pl.ds(group * TAPS, TAPS)
        return [
            send(
                ps.at[taps, (p + i) % 4], pr.at[i - 1, taps],
                rp_s.at[group, i - 1], rp_r.at[group, i - 1], p_peers[i - 1],
            )
            for i in range(1, 4)
        ]

    q_copies = []
    twin_copy = products(0)
    for group in range(1, GROUPS):
        next_copy = products(group)
        q_copies.append(chip_sum(group - 1, twin_copy))
        twin_copy = next_copy
    q_copies.append(chip_sum(GROUPS - 1, twin_copy))

    for copy in z_gather:
        copy.wait_recv()
    wb_own[:, q, p] = zb[...].astype(BF16)
    p_gather = [
        send(wb_own.at[:, q, p], wb_own.at[:, q, p], p_s.at[i], p_r.at[i], peer)
        for i, peer in enumerate(p_peers)
    ]
    p_copies = [q_sum(0, q_copies[0])]
    for copy in p_gather:
        copy.wait_recv()
    q_gather = [
        send(wb_own.at[:, q], wb_own.at[:, q], q_s.at[i], q_r.at[i], peer)
        for i, peer in enumerate(q_peers)
    ]
    d_gather = [send(wb_own.at[:, q], wb_oth.at[:, q], d_s.at[0], d_r.at[0], twin)]
    for group in range(1, GROUPS):
        p_copies.append(q_sum(group, q_copies[group]))
    for group in range(GROUPS):
        for copy in p_copies[group]:
            copy.wait_recv()

    def p_sum(k, carry):
        zs[k] = t1[k, p] + pr[0, k].astype(F32) + pr[1, k].astype(F32) + pr[2, k].astype(F32)
        return carry

    lax.fori_loop(0, K, p_sum, 0)
    z_scatter = [
        send(
            zs.at[:, pl.ds(2 * ((z + i) % 8), 2), :], zr.at[i - 1, :, pl.ds(2 * ((z + i) % 8), 2), :],
            rz_s.at[i - 1], rz_r.at[i - 1], z_peers[i - 1],
        )
        for i in range(1, 8)
    ]

    for i in range(1, 4):
        q_gather[i - 1].wait_recv()
        from_q = (q + 4 - i) % 4
        d_gather.append(
            send(wb_own.at[:, from_q], wb_oth.at[:, from_q], d_s.at[i], d_r.at[i], twin)
        )

    def input_own(m, carry):
        rows = pl.ds(pl.multiple_of(m * 256, 256), 256)
        total = jnp.zeros((256, 256), F32)
        for k in range(K):
            total = total + dot(rk[k, rows, 0:256], wb_own[k].reshape(256, 256), 1, 1)
        acc[rows, :] = total
        return carry

    lax.fori_loop(0, 4, input_own, 0)

    for copy in z_scatter:
        copy.wait_recv()
    for row, place in enumerate((2 * z + c, 2 * z + 1 - c)):
        total = zs[:, pl.ds(place, 1), :]
        for i in range(7):
            total = total + zr[i, :, pl.ds(place, 1), :]
        for k in range(K):
            fs[row, k : k + 1, :] = total[k]
    final = [
        send(fs.at[1], fr.at[0], f_s.at[0], f_r.at[0], twin),
        send(fs.at[0], fr.at[1], f_s.at[1], f_r.at[1], mirror_a),
        send(fs.at[1], fr.at[2], f_s.at[2], f_r.at[2], mirror_b),
    ]

    for copy in d_gather:
        copy.wait_recv()

    def other_weight(k):
        return jnp.concatenate([wb_oth[k, b, a] for a in range(4) for b in range(4)], axis=0)

    def input_oth(m, carry):
        rows = pl.ds(pl.multiple_of(m * 256, 256), 256)
        total = acc[rows, :]
        for k in range(K):
            total = total + dot(rk[k, rows, 256:512], other_weight(k), 1, 1)
        acc[rows, :] = total
        return carry

    lax.fori_loop(0, 4, input_oth, 0)
    stores = []
    for seq in range(2):
        eo[:, 0:256] = acc[seq * 256 : seq * 256 + 256, :].astype(BF16)
        eo[:, 256:512] = acc[512 + seq * 256 : 768 + seq * 256, :].astype(BF16)
        gi[seq] = dot(eo[...], sv[...], 1, 0).astype(BF16)
        store = pltpu.make_async_copy(gi.at[seq], gi_hbm.at[seq], store_sem.at[seq])
        store.start()
        stores.append(store)

    for copy in final:
        copy.wait_recv()
    ow[0, 0] = fs[0]
    ow[1, 0] = fr[0]
    for half in range(2):
        value = fr[1 + half]
        high = value.astype(BF16)
        rest = value - high.astype(F32)
        mid = rest.astype(BF16)
        low = (rest - mid.astype(F32)).astype(BF16)
        reverse = dot(high, flip, 1, 0) + dot(mid, flip, 1, 0) + dot(low, flip, 1, 0)
        for k in range(K):
            ow[half, 1, k : k + 1, :] = reverse[8 - k : 9 - k]
    for half, lanes in enumerate((own_lanes, oth_lanes)):
        store = pltpu.make_async_copy(ow.at[half], gw_hbm.at[:, :, lanes], store_sem.at[2 + half])
        store.start()
        stores.append(store)
    for copy in sends:
        copy.wait_send()
    for store in stores:
        store.wait()


def on_device(inputs, pre_act, grad_out, weight):
    sorts = jnp.asarray(channel_orders())
    dma = pltpu.SemaphoreType.DMA
    vmem = pltpu.VMEM
    return pl.pallas_call(
        kernel,
        out_shape=(
            jax.ShapeDtypeStruct((2, 256, 512), BF16),
            jax.ShapeDtypeStruct((2, K, 512), F32),
        ),
        in_specs=[pl.BlockSpec(memory_space=vmem)] + [pl.BlockSpec(memory_space=pl.ANY)] * 4,
        out_specs=[pl.BlockSpec(memory_space=pl.ANY)] * 2,
        scratch_shapes=[
            vmem((2, 2, 256, 256), BF16),
            vmem((2, 2, 256, 256), BF16),
            vmem((2, 256, 512), BF16),
            vmem((512, 512), BF16),
            vmem((2, 256 + 2 * HALO, 512), F32),
            vmem((2, 256 + 2 * HALO, 512), F32),
            vmem((256, 1024), BF16),
            vmem((K, 1024, 512), BF16),
            vmem((2, 2, HALO, 512), F32),
            vmem((2, 2, HALO, 512), F32),
            vmem((3, K, 256), F32),
            vmem((3, K, 256), F32),
            vmem((K, 16, 256), F32),
            vmem((K, 4, 4, 16, 256), BF16),
            vmem((K, 4, 4, 16, 256), BF16),
            vmem((K, 4, 4, 16, 256), F32),
            vmem((K, 4, 4, 16, 256), BF16),
            vmem((K, 4, 4, 16, 256), BF16),
            vmem((K, 4, 4, 16, 256), BF16),
            vmem((3, K, 4, 16, 256), BF16),
            vmem((K, 4, 16, 256), F32),
            vmem((K, 4, 16, 256), BF16),
            vmem((3, K, 16, 256), BF16),
            vmem((K, 16, 256), F32),
            vmem((7, K, 16, 256), F32),
            vmem((2, K, 256), F32),
            vmem((3, K, 256), F32),
            vmem((2, 2, K, 256), F32),
            vmem((1024, 256), F32),
            vmem((256, 512), BF16),
            vmem((2, 256, 512), BF16),
            dma((6,)), dma((4,)),
            dma((3,)), dma((3,)), dma((2,)), dma((2,)), dma((7,)), dma((7,)),
            dma((3,)), dma((3,)), dma((3,)), dma((3,)), dma((4,)), dma((4,)),
            dma((GROUPS,)), dma((GROUPS,)), dma((GROUPS, 3)), dma((GROUPS, 3)),
            dma((GROUPS, 3)), dma((GROUPS, 3)), dma((7,)), dma((7,)), dma((3,)), dma((3,)),
        ],
        compiler_params=pltpu.CompilerParams(
            collective_id=0, has_side_effects=True, vmem_limit_bytes=56 << 20
        ),
        name="conv_backward",
    )(weight, pre_act, grad_out, inputs, sorts)


def solution(mesh):
    placed = (
        P("dp", "pos", None),
        P("dp", "pos", None),
        P("dp", "pos", None),
        P(("dp", "pos"), None, None),
    )
    return jax.shard_map(
        on_device,
        mesh=mesh,
        in_specs=placed,
        out_specs=(P("dp", "pos", None), P(("dp", "pos"), None, None)),
        check_vma=False,
    )
```

```python
import jax
import jax.numpy as jnp
import numpy as np
from jax import lax
from jax.experimental import pallas as pl
from jax.experimental.pallas import tpu as pltpu
from jax.sharding import PartitionSpec as P

K = 9
HALO = 8
GROUPS = 3
TAPS = K // GROUPS
MESH = pl.DeviceIdType.MESH
F32 = jnp.float32
BF16 = jnp.bfloat16


def gelu_slope(values):
    cdf = 0.5 * (1.0 + lax.erf(values * 0.7071067811865476))
    return cdf + values * jnp.exp(-0.5 * values * values) * 0.3989422804014327


def device(x, y, z, c):
    return ((y * 4 + z % 4) * 2 + c, (z // 4) * 4 + x)


def channel_orders():
    sorts = np.zeros((2, 512, 512), np.float32)
    for core in range(2):
        for q in range(4):
            for p in range(4):
                x, y = (p, q) if core == 0 else (q, p)
                for z in range(8):
                    for c in range(2):
                        row = (q * 4 + p) * 16 + 2 * z + c
                        dp, pos = device(x, y, z, c)
                        even = 2 * (dp * 8 + pos)
                        sorts[core, row, even] = 1.0
                        sorts[core, 256 + row, 511 - even] = 1.0
    return sorts.astype(jnp.bfloat16)


def dot(a, b, ca, cb):
    return lax.dot_general(a, b, (((ca,), (cb,)), ((), ())), preferred_element_type=F32)


def kernel(
    w_ref, pre_hbm, go_hbm, x_hbm, sort_hbm, gi_hbm, gw_hbm,
    pv, gv, xv, sv, gp, gfp, xt, xe, x_out, x_in, rk, edge_out, edge_in, edge_pad, edge_rows,
    mirror_out, mirror_in, zb, wb_own, wb_oth,
    sf, sd, dr, qs, qr, t1, ps, pr, zs, zr, fs, fr, ow, acc, eo, gi,
    load_sem, store_sem, m_s, m_r, h_s, h_r, x_s, x_r, z_s, z_r, p_s, p_r, q_s, q_r, d_s, d_r,
    rd_s, rd_r, rq_s, rq_r, rp_s, rp_r, rz_s, rz_r, f_s, f_r,
):
    dp, pos = lax.axis_index("dp"), lax.axis_index("pos")
    y, c = dp // 8, dp % 2
    x = pos % 4
    z = (pos // 4) * 4 + (dp // 2) % 4
    p = x * (1 - c) + y * c
    q = y * (1 - c) + x * c
    z_steps = (4, 3, 5, 2, 6, 1, 7)
    z_peers = [device(x, y, (z + i) % 8, c) for i in z_steps]
    p_peers = [device((x + i * (1 - c)) % 4, (y + i * c) % 4, z, c) for i in range(1, 4)]
    q_peers = [device((x + i * c) % 4, (y + i * (1 - c)) % 4, z, c) for i in range(1, 4)]
    twin = device(x, y, z, 1 - c)
    mirror_a = device(3 - x, 3 - y, 7 - z, 1 - c)
    mirror_b = device(3 - x, 3 - y, 7 - z, c)
    other = dp + 1 - 2 * c
    beside = [(row, place) for place in ((pos + 1) % 8, (pos + 7) % 8) for row in (dp, other)]

    barrier = pltpu.get_barrier_semaphore()
    peers = [mirror_a, mirror_b] + beside + z_peers + p_peers + q_peers + [twin]
    for peer in peers:
        pl.semaphore_signal(barrier, inc=1, device_id=peer, device_id_type=MESH)

    own_lanes = pl.ds(pl.multiple_of(c * 256, 256), 256)
    oth_lanes = pl.ds(pl.multiple_of((1 - c) * 256, 256), 256)
    loads = [
        pltpu.make_async_copy(pre_hbm.at[:, :, own_lanes], pv.at[0], load_sem.at[0]),
        pltpu.make_async_copy(go_hbm.at[:, :, own_lanes], gv.at[0], load_sem.at[1]),
        pltpu.make_async_copy(pre_hbm.at[:, :, oth_lanes], pv.at[1], load_sem.at[2]),
        pltpu.make_async_copy(go_hbm.at[:, :, oth_lanes], gv.at[1], load_sem.at[3]),
        pltpu.make_async_copy(x_hbm, xv, load_sem.at[4]),
        pltpu.make_async_copy(sort_hbm.at[c], sv, load_sem.at[5]),
    ]
    for load in loads:
        load.start()

    sends = []

    def send(src, dst, send_sem, recv_sem, peer):
        copy = pltpu.make_async_remote_copy(
            src_ref=src, dst_ref=dst, send_sem=send_sem, recv_sem=recv_sem,
            device_id=peer, device_id_type=MESH,
        )
        copy.start()
        sends.append(copy)
        return copy

    rows_i = lax.broadcasted_iota(jnp.int32, (256, 256), 0)
    cols_i = lax.broadcasted_iota(jnp.int32, (256, 256), 1)
    flip = jnp.where(rows_i + cols_i == 255, 1.0, 0.0).astype(BF16)

    w_own = w_ref[:, :, own_lanes].astype(F32)
    w_oth = w_ref[:, :, oth_lanes].astype(F32)
    w0_own = w_own[:, 0, :]
    for i, row in enumerate((w_own[:, 1, :], w_oth[:, 1, :], w_oth[:, 0, :])):
        mirror_out[i] = jnp.concatenate([row, jnp.zeros((16 - K, 256), F32)], axis=0).astype(BF16)

    zeros = jnp.zeros((2, HALO, 512), F32)
    for padded in (gp, gfp):
        padded[:, 0:HALO, :] = zeros
        padded[:, HALO + 256 : 2 * HALO + 256, :] = zeros
    for half in range(2):
        loads[2 * half].wait()
        loads[2 * half + 1].wait()
        for seq in range(2):

            def slope(i, carry, half=half, seq=seq):
                rows = pl.ds(pl.multiple_of(i * 32, 32), 32)
                values = pv[half, seq, rows, :].astype(F32)
                grad = gv[half, seq, rows, :].astype(F32) * gelu_slope(values)
                place = pl.ds(pl.multiple_of(HALO + i * 32, 8), 32)
                gp[seq, place, half * 256 : half * 256 + 256] = grad.astype(BF16).astype(F32)
                return carry

            lax.fori_loop(0, 8, slope, 0)
    edge_out[0] = gp[:, 256 : 256 + HALO, :].reshape(2 * HALO, 512).astype(BF16)
    edge_out[1] = gp[:, HALO : 2 * HALO, :].reshape(2 * HALO, 512).astype(BF16)

    for seq in range(2):
        main = gp[seq, HALO : HALO + 256, :].astype(BF16)
        gfp[seq, HALO : HALO + 256, 0:256] = dot(main[:, 256:512], flip, 1, 0)
        gfp[seq, HALO : HALO + 256, 256:512] = dot(main[:, 0:256], flip, 1, 0)
    loads[4].wait()
    loads[5].wait()
    for seq in range(2):
        sorted_x = dot(sv[...], xv[seq], 1, 1).astype(BF16)
        xt[:, seq * 256 : seq * 256 + 256] = sorted_x[0:256]
        xt[:, 512 + seq * 256 : 768 + seq * 256] = sorted_x[256:512]
    for k in range(K):
        for seq in range(2):
            rk[k, seq * 256 : seq * 256 + 256, :] = gp[seq, 12 - k : 268 - k, :].astype(BF16)
            rk[k, 512 + seq * 256 : 768 + seq * 256, :] = gfp[seq, 4 + k : 260 + k, :].astype(BF16)

    for end, start in enumerate((0, 248)):
        ends = [xv[seq, start : start + 8, :].astype(F32) for seq in range(2)]
        x_out[end] = jnp.concatenate(ends, axis=0).astype(BF16)

    pl.semaphore_wait(barrier, len(peers))
    mirror = [
        send(mirror_out.at[i], mirror_in.at[i], m_s.at[i], m_r.at[i], peer)
        for i, peer in enumerate((mirror_a, mirror_b, twin))
    ]
    edges = [
        pltpu.make_async_remote_copy(
            src_ref=edge_out.at[i // 2], dst_ref=edge_in.at[i],
            send_sem=h_s.at[i], recv_sem=h_r.at[i],
            device_id=peer, device_id_type=MESH,
        )
        for i, peer in enumerate(beside)
    ]
    last_pos, first_pos = pos == 7, pos == 0
    for side, at_end in enumerate((last_pos, first_pos)):

        @pl.when(jnp.logical_not(at_end))
        def _(side=side):
            edges[2 * side].start()
            edges[2 * side + 1].start()

    x_ends = send(x_out, x_in, x_s.at[0], x_r.at[0], twin)

    def inner(k, carry):
        terms = dot(xt[...], rk[k], 1, 0)
        sf[k] = terms[:, 0:256].reshape(4, 4, 16, 256)
        for a in range(4):
            for b in range(4):
                rows = slice((a * 4 + b) * 16, (a * 4 + b) * 16 + 16)
                sd[k, b, a] = terms[rows, 256:512].astype(BF16)
        return carry

    twin_copies = []
    for group in range(GROUPS):
        lax.fori_loop(group * TAPS, group * TAPS + TAPS, inner, 0, unroll=True)
        taps = pl.ds(group * TAPS, TAPS)
        twin_copies.append(send(sd.at[taps], dr.at[taps], rd_s.at[group], rd_r.at[group], twin))

    for copy in mirror:
        copy.wait_recv()
    rev_a = dot(mirror_in[0], flip, 1, 0)
    rev_b = dot(mirror_in[1], flip, 1, 0)
    w0_oth = mirror_in[2].astype(F32)
    for k in range(K):
        zb[k, pl.ds(2 * z + c, 1), :] = w0_own[k : k + 1] + rev_a[8 - k : 9 - k]
        zb[k, pl.ds(2 * z + 1 - c, 1), :] = w0_oth[k : k + 1] + rev_b[8 - k : 9 - k]
    mine = pl.ds(2 * z, 2)
    z_gather = [
        send(zb.at[:, mine, :], zb.at[:, mine, :], z_s.at[i], z_r.at[i], peer)
        for i, peer in enumerate(z_peers)
    ]

    x_ends.wait_recv()
    blank = jnp.zeros((32, 512), BF16)
    for i in range(2):
        even_rows = jnp.concatenate([x_out[1 - i], x_in[1 - i], blank], axis=0)
        odd_rows = jnp.concatenate([blank, x_out[i], x_in[i]], axis=0)
        xe[i] = (dot(sv[0:256, :], even_rows, 1, 1) + dot(sv[256:512, :], odd_rows, 1, 1)).astype(BF16)
    for side, at_end in enumerate((first_pos, last_pos)):

        @pl.when(jnp.logical_not(at_end))
        def _(side=side):
            edges[2 * side].wait_recv()
            edges[2 * side + 1].wait_recv()

    border = [
        [jnp.where(at_end, 0.0, edge_in[2 * side + core].astype(F32)) for core in range(2)]
        for side, at_end in enumerate((first_pos, last_pos))
    ]
    low, high = [
        [
            border[side][core][seq * HALO : seq * HALO + HALO, core * 256 : core * 256 + 256]
            for core in range(2)
            for seq in range(2)
        ]
        for side in range(2)
    ]
    reverse_of = jnp.concatenate(
        [
            border[side][core][:, 256 - core * 256 : 512 - core * 256]
            for side in range(2)
            for core in range(2)
        ],
        axis=0,
    ).astype(BF16)
    reverse_of = dot(reverse_of, flip, 1, 0)
    blank = jnp.zeros((HALO, 256), F32)
    for seq in range(4):
        rev_low = reverse_of[seq * HALO : seq * HALO + HALO]
        rev_high = reverse_of[(4 + seq) * HALO : (5 + seq) * HALO]
        for i, parts in enumerate(
            ((blank, high[seq]), (rev_low, blank), (low[seq], blank), (blank, rev_high))
        ):
            edge_pad[i, seq, 0:HALO, :] = parts[0]
            edge_pad[i, seq, HALO : 2 * HALO, :] = parts[1]
    for k in range(K):
        first, second = (0, 1) if k <= 4 else (2, 3)
        start_1, start_2 = (4 - k, 4 + k) if k <= 4 else (12 - k, k - 4)
        rows_1 = [edge_pad[first, seq, start_1 : start_1 + 8, :] for seq in range(4)]
        rows_2 = [edge_pad[second, seq, start_2 : start_2 + 8, :] for seq in range(4)]
        edge_rows[k] = jnp.concatenate(rows_1 + rows_2, axis=0).astype(BF16)

    def chip_sum(group):
        twin_copies[group].wait_recv()

        def one(k, carry):
            terms = dot(xe[k // 5], edge_rows[k], 1, 0).reshape(4, 4, 16, 256)
            total = sf[k] + dr[k].astype(F32) + terms
            sf[k] = total
            qs[k] = total.astype(BF16)
            return carry

        lax.fori_loop(group * TAPS, group * TAPS + TAPS, one, 0)
        taps = pl.ds(group * TAPS, TAPS)
        return [
            send(
                qs.at[taps, (q + i) % 4], qr.at[i - 1, taps],
                rq_s.at[group, i - 1], rq_r.at[group, i - 1], q_peers[i - 1],
            )
            for i in range(1, 4)
        ]

    def q_sum(group, copies):
        for copy in copies:
            copy.wait_recv()

        def one(k, carry):
            total = sf[k, q] + qr[0, k].astype(F32) + qr[1, k].astype(F32) + qr[2, k].astype(F32)
            t1[k] = total
            ps[k] = total.astype(BF16)
            return carry

        lax.fori_loop(group * TAPS, group * TAPS + TAPS, one, 0)
        taps = pl.ds(group * TAPS, TAPS)
        return [
            send(
                ps.at[taps, (p + i) % 4], pr.at[i - 1, taps],
                rp_s.at[group, i - 1], rp_r.at[group, i - 1], p_peers[i - 1],
            )
            for i in range(1, 4)
        ]

    q_copies = [chip_sum(group) for group in range(GROUPS)]

    low = jnp.where(first_pos, 0.0, edge_in[0].astype(F32)).reshape(2, HALO, 512)
    high = jnp.where(last_pos, 0.0, edge_in[2].astype(F32)).reshape(2, HALO, 512)
    gp[:, 0:HALO, :] = low
    gp[:, HALO + 256 : 2 * HALO + 256, :] = high
    both = jnp.concatenate([low[0], low[1], high[0], high[1]], axis=0).astype(BF16)
    both = jnp.concatenate(
        [dot(both[:, 256:512], flip, 1, 0), dot(both[:, 0:256], flip, 1, 0)], axis=1
    )
    for seq in range(2):
        gfp[seq, 0:HALO, :] = both[seq * HALO : seq * HALO + HALO]
        gfp[seq, HALO + 256 : 2 * HALO + 256, :] = both[(2 + seq) * HALO : (3 + seq) * HALO]
    for k in range(K):
        for seq in range(2):
            for start in (0, 240):
                rk[k, seq * 256 + start : seq * 256 + start + 16, :] = gp[
                    seq, 12 - k + start : 28 - k + start, :
                ].astype(BF16)
                rk[k, 512 + seq * 256 + start : 528 + seq * 256 + start, :] = gfp[
                    seq, 4 + k + start : 20 + k + start, :
                ].astype(BF16)

    for copy in z_gather:
        copy.wait_recv()
    wb_own[:, q, p] = zb[...].astype(BF16)
    p_gather = [
        send(wb_own.at[:, q, p], wb_own.at[:, q, p], p_s.at[i], p_r.at[i], peer)
        for i, peer in enumerate(p_peers)
    ]
    p_copies = [q_sum(group, q_copies[group]) for group in range(GROUPS)]
    for copy in p_gather:
        copy.wait_recv()
    q_gather = [
        send(wb_own.at[:, q], wb_own.at[:, q], q_s.at[i], q_r.at[i], peer)
        for i, peer in enumerate(q_peers)
    ]
    d_gather = [send(wb_own.at[:, q], wb_oth.at[:, q], d_s.at[0], d_r.at[0], twin)]
    def p_sum(k, carry):
        zs[k] = t1[k, p] + pr[0, k].astype(F32) + pr[1, k].astype(F32) + pr[2, k].astype(F32)
        return carry

    z_scatter = []
    for group in range(GROUPS):
        for copy in p_copies[group]:
            copy.wait_recv()
        lax.fori_loop(group * TAPS, group * TAPS + TAPS, p_sum, 0)
        taps = pl.ds(group * TAPS, TAPS)
        for i, step in enumerate(z_steps):
            rows = pl.ds(2 * ((z + step) % 8), 2)
            z_scatter.append(
                send(
                    zs.at[taps, rows, :], zr.at[i, taps, rows, :],
                    rz_s.at[group, i], rz_r.at[group, i], z_peers[i],
                )
            )

    for i in range(1, 4):
        q_gather[i - 1].wait_recv()
        from_q = (q + 4 - i) % 4
        d_gather.append(
            send(wb_own.at[:, from_q], wb_oth.at[:, from_q], d_s.at[i], d_r.at[i], twin)
        )

    for copy in z_scatter:
        copy.wait_recv()
    for row, place in enumerate((2 * z + c, 2 * z + 1 - c)):
        total = zs[:, pl.ds(place, 1), :]
        for i in range(7):
            total = total + zr[i, :, pl.ds(place, 1), :]
        fs[row, 8:16, :] = jnp.zeros((8, 256), F32)
        for k in range(K):
            fs[row, k : k + 1, :] = total[k]
    final = [
        send(fs.at[1], fr.at[0], f_s.at[0], f_r.at[0], twin),
        send(fs.at[0], fr.at[1], f_s.at[1], f_r.at[1], mirror_a),
        send(fs.at[1], fr.at[2], f_s.at[2], f_r.at[2], mirror_b),
    ]

    total = jnp.zeros((1024, 256), F32)
    for k in range(K):
        total = total + dot(rk[k, :, 0:256], wb_own[k].reshape(256, 256), 1, 1)
    acc[...] = total

    for copy in d_gather:
        copy.wait_recv()

    def other_weight(k):
        return jnp.concatenate([wb_oth[k, b, a] for a in range(4) for b in range(4)], axis=0)

    total = acc[...]
    for k in range(K):
        total = total + dot(rk[k, :, 256:512], other_weight(k), 1, 1)
    acc[...] = total
    stores = []
    for seq in range(2):
        eo[:, 0:256] = acc[seq * 256 : seq * 256 + 256, :].astype(BF16)
        eo[:, 256:512] = acc[512 + seq * 256 : 768 + seq * 256, :].astype(BF16)
        gi[seq] = dot(eo[...], sv[...], 1, 0).astype(BF16)
        store = pltpu.make_async_copy(gi.at[seq], gi_hbm.at[seq], store_sem.at[seq])
        store.start()
        stores.append(store)

    for copy in final:
        copy.wait_recv()
    ow[0, :, 0, :] = fs[0, 0:K, :]
    ow[1, :, 0, :] = fr[0, 0:K, :]
    for half in range(2):
        value = fr[1 + half]
        high = value.astype(BF16)
        rest = value - high.astype(F32)
        mid = rest.astype(BF16)
        low = (rest - mid.astype(F32)).astype(BF16)
        reverse = dot(high, flip, 1, 0) + dot(mid, flip, 1, 0) + dot(low, flip, 1, 0)
        for k in range(K):
            ow[half, k, 1:2, :] = reverse[8 - k : 9 - k]
    for half, lanes in enumerate((own_lanes, oth_lanes)):
        store = pltpu.make_async_copy(ow.at[half], gw_hbm.at[:, :, lanes], store_sem.at[2 + half])
        store.start()
        stores.append(store)
    for copy in sends:
        copy.wait_send()
    for side, at_end in enumerate((last_pos, first_pos)):

        @pl.when(jnp.logical_not(at_end))
        def _(side=side):
            edges[2 * side].wait_send()
            edges[2 * side + 1].wait_send()

    for store in stores:
        store.wait()


def store_kernel(gi_in, gw_in, gi_out, gw_out):
    gi_out[...] = gi_in[...]
    gw_out[...] = gw_in[...]


def on_device(inputs, pre_act, grad_out, weight):
    sorts = jnp.asarray(channel_orders())
    dma = pltpu.SemaphoreType.DMA
    vmem = pltpu.VMEM
    grad_input, grad_weight = pl.pallas_call(
        kernel,
        out_shape=(
            jax.ShapeDtypeStruct((2, 256, 512), BF16),
            jax.ShapeDtypeStruct((K, 2, 512), F32),
        ),
        in_specs=[pl.BlockSpec(memory_space=vmem)] + [pl.BlockSpec(memory_space=pl.ANY)] * 4,
        out_specs=[pl.BlockSpec(memory_space=pl.ANY)] * 2,
        scratch_shapes=[
            vmem((2, 2, 256, 256), BF16),
            vmem((2, 2, 256, 256), BF16),
            vmem((2, 256, 512), BF16),
            vmem((512, 512), BF16),
            vmem((2, 256 + 2 * HALO, 512), F32),
            vmem((2, 256 + 2 * HALO, 512), F32),
            vmem((256, 1024), BF16),
            vmem((2, 256, 64), BF16),
            vmem((2, 16, 512), BF16),
            vmem((2, 16, 512), BF16),
            vmem((K, 1024, 512), BF16),
            vmem((2, 2 * HALO, 512), BF16),
            vmem((4, 2 * HALO, 512), BF16),
            vmem((4, 4, 2 * HALO, 256), F32),
            vmem((K, 64, 256), BF16),
            vmem((3, 16, 256), BF16),
            vmem((3, 16, 256), BF16),
            vmem((K, 16, 256), F32),
            vmem((K, 4, 4, 16, 256), BF16),
            vmem((K, 4, 4, 16, 256), BF16),
            vmem((K, 4, 4, 16, 256), F32),
            vmem((K, 4, 4, 16, 256), BF16),
            vmem((K, 4, 4, 16, 256), BF16),
            vmem((K, 4, 4, 16, 256), BF16),
            vmem((3, K, 4, 16, 256), BF16),
            vmem((K, 4, 16, 256), F32),
            vmem((K, 4, 16, 256), BF16),
            vmem((3, K, 16, 256), BF16),
            vmem((K, 16, 256), F32),
            vmem((7, K, 16, 256), F32),
            vmem((2, 16, 256), F32),
            vmem((3, 16, 256), F32),
            vmem((2, K, 2, 256), F32),
            vmem((1024, 256), F32),
            vmem((256, 512), BF16),
            vmem((2, 256, 512), BF16),
            dma((6,)), dma((4,)),
            dma((3,)), dma((3,)), dma((4,)), dma((4,)), dma((1,)), dma((1,)), dma((7,)), dma((7,)),
            dma((3,)), dma((3,)), dma((3,)), dma((3,)), dma((4,)), dma((4,)),
            dma((GROUPS,)), dma((GROUPS,)), dma((GROUPS, 3)), dma((GROUPS, 3)),
            dma((GROUPS, 3)), dma((GROUPS, 3)), dma((GROUPS, 7)), dma((GROUPS, 7)), dma((3,)), dma((3,)),
        ],
        compiler_params=pltpu.CompilerParams(
            collective_id=0, has_side_effects=True, vmem_limit_bytes=56 << 20
        ),
        name="conv_backward",
    )(jnp.transpose(weight, (1, 0, 2)), pre_act, grad_out, inputs, sorts)
    grad_input, grad_weight = pl.pallas_call(
        store_kernel,
        out_shape=(
            jax.ShapeDtypeStruct((2, 256, 512), BF16),
            jax.ShapeDtypeStruct((K, 2, 512), F32),
        ),
        in_specs=[pl.BlockSpec(memory_space=vmem)] * 2,
        out_specs=[pl.BlockSpec(memory_space=vmem)] * 2,
        name="store",
    )(grad_input, grad_weight)
    return grad_input, jnp.transpose(grad_weight, (1, 0, 2))


def solution(mesh):
    placed = (
        P("dp", "pos", None),
        P("dp", "pos", None),
        P("dp", "pos", None),
        P(("dp", "pos"), None, None),
    )
    return jax.shard_map(
        on_device,
        mesh=mesh,
        in_specs=placed,
        out_specs=(P("dp", "pos", None), P(("dp", "pos"), None, None)),
        check_vma=False,
    )
```

```python
import jax
import jax.numpy as jnp
import numpy as np
from jax import lax
from jax.experimental import pallas as pl
from jax.experimental.pallas import tpu as pltpu
from jax.sharding import PartitionSpec as P

K = 9
HALO = 8
GROUPS = 3
TAPS = K // GROUPS
MESH = pl.DeviceIdType.MESH
F32 = jnp.float32
BF16 = jnp.bfloat16


def gelu_slope(values):
    cdf = 0.5 * (1.0 + lax.erf(values * 0.7071067811865476))
    return cdf + values * jnp.exp(-0.5 * values * values) * 0.3989422804014327


def device(x, y, z, c):
    return ((y * 4 + z % 4) * 2 + c, (z // 4) * 4 + x)


def channel_orders():
    sorts = np.zeros((2, 512, 512), np.float32)
    for core in range(2):
        for q in range(4):
            for p in range(4):
                x, y = (p, q) if core == 0 else (q, p)
                for z in range(8):
                    for c in range(2):
                        row = (q * 4 + p) * 16 + 2 * z + c
                        dp, pos = device(x, y, z, c)
                        even = 2 * (dp * 8 + pos)
                        sorts[core, row, even] = 1.0
                        sorts[core, 256 + row, 511 - even] = 1.0
    return sorts.astype(jnp.bfloat16)


def dot(a, b, ca, cb):
    return lax.dot_general(a, b, (((ca,), (cb,)), ((), ())), preferred_element_type=F32)


def kernel(
    w_hbm, pre_hbm, go_hbm, x_hbm, sort_hbm, gi, gw,
    w_ref, pv, gv, xv, sv, gp, gfp, xt, xe, x_out, x_in, rk, edge_out, edge_in, edge_pad, edge_rows,
    mirror_out, mirror_in, zb, wb_own, wb_oth,
    sf, sd, dr, qs, qr, t1, ps, pr, zs, zr, fs, fr, acc, eo,
    load_sem, m_s, m_r, h_s, h_r, x_s, x_r, z_s, z_r, p_s, p_r, q_s, q_r, d_s, d_r,
    rd_s, rd_r, rq_s, rq_r, rp_s, rp_r, rz_s, rz_r, f_s, f_r,
):
    dp, pos = lax.axis_index("dp"), lax.axis_index("pos")
    y, c = dp // 8, dp % 2
    x = pos % 4
    z = (pos // 4) * 4 + (dp // 2) % 4
    p = x * (1 - c) + y * c
    q = y * (1 - c) + x * c
    z_steps = (4, 3, 5, 2, 6, 1, 7)
    z_peers = [device(x, y, (z + i) % 8, c) for i in z_steps]
    p_peers = [device((x + i * (1 - c)) % 4, (y + i * c) % 4, z, c) for i in range(1, 4)]
    q_peers = [device((x + i * c) % 4, (y + i * (1 - c)) % 4, z, c) for i in range(1, 4)]
    twin = device(x, y, z, 1 - c)
    mirror_a = device(3 - x, 3 - y, 7 - z, 1 - c)
    mirror_b = device(3 - x, 3 - y, 7 - z, c)
    other = dp + 1 - 2 * c
    beside = [(row, place) for place in ((pos + 1) % 8, (pos + 7) % 8) for row in (dp, other)]

    barrier = pltpu.get_barrier_semaphore()
    peers = [mirror_a, mirror_b] + beside + z_peers + p_peers + q_peers + [twin]
    for peer in peers:
        pl.semaphore_signal(barrier, inc=1, device_id=peer, device_id_type=MESH)

    own_lanes = pl.ds(pl.multiple_of(c * 256, 256), 256)
    oth_lanes = pl.ds(pl.multiple_of((1 - c) * 256, 256), 256)
    loads = [
        pltpu.make_async_copy(pre_hbm.at[:, :, own_lanes], pv.at[0], load_sem.at[0]),
        pltpu.make_async_copy(go_hbm.at[:, :, own_lanes], gv.at[0], load_sem.at[1]),
        pltpu.make_async_copy(pre_hbm.at[:, :, oth_lanes], pv.at[1], load_sem.at[2]),
        pltpu.make_async_copy(go_hbm.at[:, :, oth_lanes], gv.at[1], load_sem.at[3]),
        pltpu.make_async_copy(x_hbm, xv, load_sem.at[4]),
        pltpu.make_async_copy(sort_hbm.at[c], sv, load_sem.at[5]),
        pltpu.make_async_copy(w_hbm, w_ref, load_sem.at[6]),
    ]
    for load in loads:
        load.start()

    sends = []

    def drain():
        while sends:
            sends.pop(0).wait_send()


    def send(src, dst, send_sem, recv_sem, peer):
        copy = pltpu.make_async_remote_copy(
            src_ref=src, dst_ref=dst, send_sem=send_sem, recv_sem=recv_sem,
            device_id=peer, device_id_type=MESH,
        )
        copy.start()
        sends.append(copy)
        return copy

    rows_i = lax.broadcasted_iota(jnp.int32, (256, 256), 0)
    cols_i = lax.broadcasted_iota(jnp.int32, (256, 256), 1)
    flip = jnp.where(rows_i + cols_i == 255, 1.0, 0.0).astype(BF16)

    zeros = jnp.zeros((2, HALO, 512), F32)
    for padded in (gp, gfp):
        padded[:, 0:HALO, :] = zeros
        padded[:, HALO + 256 : 2 * HALO + 256, :] = zeros
    for half in range(2):
        loads[2 * half].wait()
        loads[2 * half + 1].wait()
        for seq in range(2):

            def slope(i, carry, half=half, seq=seq):
                rows = pl.ds(pl.multiple_of(i * 32, 32), 32)
                values = pv[half, seq, rows, :].astype(F32)
                grad = gv[half, seq, rows, :].astype(F32) * gelu_slope(values)
                place = pl.ds(pl.multiple_of(HALO + i * 32, 8), 32)
                gp[seq, place, half * 256 : half * 256 + 256] = grad.astype(BF16).astype(F32)
                return carry

            lax.fori_loop(0, 8, slope, 0)
    loads[6].wait()
    w_own = w_ref[:, :, own_lanes].astype(F32)
    w_oth = w_ref[:, :, oth_lanes].astype(F32)
    w0_own = w_own[:, 0, :]
    for i, row in enumerate((w_own[:, 1, :], w_oth[:, 1, :], w_oth[:, 0, :])):
        mirror_out[i] = jnp.concatenate([row, jnp.zeros((16 - K, 256), F32)], axis=0).astype(BF16)

    edge_out[0] = gp[:, 256 : 256 + HALO, :].reshape(2 * HALO, 512).astype(BF16)
    edge_out[1] = gp[:, HALO : 2 * HALO, :].reshape(2 * HALO, 512).astype(BF16)

    loads[4].wait()
    for end, start in enumerate((0, 248)):
        ends = [xv[seq, start : start + 8, :].astype(F32) for seq in range(2)]
        x_out[end] = jnp.concatenate(ends, axis=0).astype(BF16)

    pl.semaphore_wait(barrier, len(peers))
    mirror = [
        send(mirror_out.at[i], mirror_in.at[i], m_s.at[i], m_r.at[i], peer)
        for i, peer in enumerate((mirror_a, mirror_b, twin))
    ]
    edges = [
        pltpu.make_async_remote_copy(
            src_ref=edge_out.at[i // 2], dst_ref=edge_in.at[i],
            send_sem=h_s.at[i], recv_sem=h_r.at[i],
            device_id=peer, device_id_type=MESH,
        )
        for i, peer in enumerate(beside)
    ]
    last_pos, first_pos = pos == 7, pos == 0
    for side, at_end in enumerate((last_pos, first_pos)):

        @pl.when(jnp.logical_not(at_end))
        def _(side=side):
            edges[2 * side].start()
            edges[2 * side + 1].start()

    x_ends = send(x_out, x_in, x_s.at[0], x_r.at[0], twin)

    for seq in range(2):
        main = gp[seq, HALO : HALO + 256, :].astype(BF16)
        gfp[seq, HALO : HALO + 256, 0:256] = dot(main[:, 256:512], flip, 1, 0)
        gfp[seq, HALO : HALO + 256, 256:512] = dot(main[:, 0:256], flip, 1, 0)
    loads[5].wait()
    for seq in range(2):
        sorted_x = dot(sv[...], xv[seq], 1, 1).astype(BF16)
        xt[:, seq * 256 : seq * 256 + 256] = sorted_x[0:256]
        xt[:, 512 + seq * 256 : 768 + seq * 256] = sorted_x[256:512]
    for k in range(K):
        for seq in range(2):
            rk[k, seq * 256 : seq * 256 + 256, :] = gp[seq, 12 - k : 268 - k, :].astype(BF16)
            rk[k, 512 + seq * 256 : 768 + seq * 256, :] = gfp[seq, 4 + k : 260 + k, :].astype(BF16)

    def inner(k, carry):
        terms = dot(xt[...], rk[k], 1, 0)
        sf[k] = terms[:, 0:256].reshape(4, 4, 16, 256)
        for a in range(4):
            for b in range(4):
                rows = slice((a * 4 + b) * 16, (a * 4 + b) * 16 + 16)
                sd[k, b, a] = terms[rows, 256:512].astype(BF16)
        return carry

    twin_copies = []
    for group in range(GROUPS):
        lax.fori_loop(group * TAPS, group * TAPS + TAPS, inner, 0, unroll=True)
        taps = pl.ds(group * TAPS, TAPS)
        twin_copies.append(send(sd.at[taps], dr.at[taps], rd_s.at[group], rd_r.at[group], twin))

    x_ends.wait_recv()
    blank = jnp.zeros((32, 512), BF16)
    for i in range(2):
        even_rows = jnp.concatenate([x_out[1 - i], x_in[1 - i], blank], axis=0)
        odd_rows = jnp.concatenate([blank, x_out[i], x_in[i]], axis=0)
        xe[i] = (dot(sv[0:256, :], even_rows, 1, 1) + dot(sv[256:512, :], odd_rows, 1, 1)).astype(BF16)
    for copy in mirror:
        copy.wait_recv()
    rev_a = dot(mirror_in[0], flip, 1, 0)
    rev_b = dot(mirror_in[1], flip, 1, 0)
    w0_oth = mirror_in[2].astype(F32)
    for k in range(K):
        zb[k, pl.ds(2 * z + c, 1), :] = w0_own[k : k + 1] + rev_a[8 - k : 9 - k]
        zb[k, pl.ds(2 * z + 1 - c, 1), :] = w0_oth[k : k + 1] + rev_b[8 - k : 9 - k]
    mine = pl.ds(2 * z, 2)
    z_gather = [
        send(zb.at[:, mine, :], zb.at[:, mine, :], z_s.at[i], z_r.at[i], peer)
        for i, peer in enumerate(z_peers)
    ]

    for side, at_end in enumerate((first_pos, last_pos)):

        @pl.when(jnp.logical_not(at_end))
        def _(side=side):
            edges[2 * side].wait_recv()
            edges[2 * side + 1].wait_recv()

    border = [
        [jnp.where(at_end, 0.0, edge_in[2 * side + core].astype(F32)) for core in range(2)]
        for side, at_end in enumerate((first_pos, last_pos))
    ]
    low, high = [
        [
            border[side][core][seq * HALO : seq * HALO + HALO, core * 256 : core * 256 + 256]
            for core in range(2)
            for seq in range(2)
        ]
        for side in range(2)
    ]
    reverse_of = jnp.concatenate(
        [
            border[side][core][:, 256 - core * 256 : 512 - core * 256]
            for side in range(2)
            for core in range(2)
        ],
        axis=0,
    ).astype(BF16)
    reverse_of = dot(reverse_of, flip, 1, 0)
    blank = jnp.zeros((HALO, 256), F32)
    for seq in range(4):
        rev_low = reverse_of[seq * HALO : seq * HALO + HALO]
        rev_high = reverse_of[(4 + seq) * HALO : (5 + seq) * HALO]
        for i, parts in enumerate(
            ((blank, high[seq]), (rev_low, blank), (low[seq], blank), (blank, rev_high))
        ):
            edge_pad[i, seq, 0:HALO, :] = parts[0]
            edge_pad[i, seq, HALO : 2 * HALO, :] = parts[1]
    for k in range(K):
        first, second = (0, 1) if k <= 4 else (2, 3)
        start_1, start_2 = (4 - k, 4 + k) if k <= 4 else (12 - k, k - 4)
        rows_1 = [edge_pad[first, seq, start_1 : start_1 + 8, :] for seq in range(4)]
        rows_2 = [edge_pad[second, seq, start_2 : start_2 + 8, :] for seq in range(4)]
        edge_rows[k] = jnp.concatenate(rows_1 + rows_2, axis=0).astype(BF16)

    def chip_sum(group):
        twin_copies[group].wait_recv()

        def one(k, carry):
            terms = dot(xe[k // 5], edge_rows[k], 1, 0).reshape(4, 4, 16, 256)
            total = sf[k] + dr[k].astype(F32) + terms
            sf[k] = total
            qs[k] = total.astype(BF16)
            return carry

        lax.fori_loop(group * TAPS, group * TAPS + TAPS, one, 0)
        taps = pl.ds(group * TAPS, TAPS)
        return [
            send(
                qs.at[taps, (q + i) % 4], qr.at[i - 1, taps],
                rq_s.at[group, i - 1], rq_r.at[group, i - 1], q_peers[i - 1],
            )
            for i in range(1, 4)
        ]

    def q_sum(group, copies):
        for copy in copies:
            copy.wait_recv()

        def one(k, carry):
            total = sf[k, q] + qr[0, k].astype(F32) + qr[1, k].astype(F32) + qr[2, k].astype(F32)
            t1[k] = total
            ps[k] = total.astype(BF16)
            return carry

        lax.fori_loop(group * TAPS, group * TAPS + TAPS, one, 0)
        taps = pl.ds(group * TAPS, TAPS)
        return [
            send(
                ps.at[taps, (p + i) % 4], pr.at[i - 1, taps],
                rp_s.at[group, i - 1], rp_r.at[group, i - 1], p_peers[i - 1],
            )
            for i in range(1, 4)
        ]

    q_copies = [chip_sum(group) for group in range(GROUPS)]

    low = jnp.where(first_pos, 0.0, edge_in[0].astype(F32)).reshape(2, HALO, 512)
    high = jnp.where(last_pos, 0.0, edge_in[2].astype(F32)).reshape(2, HALO, 512)
    gp[:, 0:HALO, :] = low
    gp[:, HALO + 256 : 2 * HALO + 256, :] = high
    both = jnp.concatenate([low[0], low[1], high[0], high[1]], axis=0).astype(BF16)
    both = jnp.concatenate(
        [dot(both[:, 256:512], flip, 1, 0), dot(both[:, 0:256], flip, 1, 0)], axis=1
    )
    for seq in range(2):
        gfp[seq, 0:HALO, :] = both[seq * HALO : seq * HALO + HALO]
        gfp[seq, HALO + 256 : 2 * HALO + 256, :] = both[(2 + seq) * HALO : (3 + seq) * HALO]
    for k in range(K):
        for seq in range(2):
            for start in (0, 240):
                rk[k, seq * 256 + start : seq * 256 + start + 16, :] = gp[
                    seq, 12 - k + start : 28 - k + start, :
                ].astype(BF16)
                rk[k, 512 + seq * 256 + start : 528 + seq * 256 + start, :] = gfp[
                    seq, 4 + k + start : 20 + k + start, :
                ].astype(BF16)

    for copy in z_gather:
        copy.wait_recv()
    wb_own[:, q, p] = zb[...].astype(BF16)
    p_gather = [
        send(wb_own.at[:, q, p], wb_own.at[:, q, p], p_s.at[i], p_r.at[i], peer)
        for i, peer in enumerate(p_peers)
    ]
    p_copies = [q_sum(group, q_copies[group]) for group in range(GROUPS)]
    for copy in p_gather:
        copy.wait_recv()
    q_gather = [
        send(wb_own.at[:, q], wb_own.at[:, q], q_s.at[i], q_r.at[i], peer)
        for i, peer in enumerate(q_peers)
    ]
    d_gather = [send(wb_own.at[:, q], wb_oth.at[:, q], d_s.at[0], d_r.at[0], twin)]
    def p_sum(k, carry):
        zs[k] = t1[k, p] + pr[0, k].astype(F32) + pr[1, k].astype(F32) + pr[2, k].astype(F32)
        return carry

    z_scatter = []
    for group in range(GROUPS):
        for copy in p_copies[group]:
            copy.wait_recv()
        lax.fori_loop(group * TAPS, group * TAPS + TAPS, p_sum, 0)
        taps = pl.ds(group * TAPS, TAPS)
        for i, step in enumerate(z_steps):
            rows = pl.ds(2 * ((z + step) % 8), 2)
            z_scatter.append(
                send(
                    zs.at[taps, rows, :], zr.at[i, taps, rows, :],
                    rz_s.at[group, i], rz_r.at[group, i], z_peers[i],
                )
            )

    for i in range(1, 4):
        q_gather[i - 1].wait_recv()
        from_q = (q + 4 - i) % 4
        d_gather.append(
            send(wb_own.at[:, from_q], wb_oth.at[:, from_q], d_s.at[i], d_r.at[i], twin)
        )

    fs[:, 8:16, :] = jnp.zeros((2, 8, 256), F32)
    for group in range(GROUPS):
        for copy in z_scatter[group * 7 : group * 7 + 7]:
            copy.wait_recv()
        taps = slice(group * TAPS, group * TAPS + TAPS)
        for row, place in enumerate((2 * z + c, 2 * z + 1 - c)):
            total = zs[taps, pl.ds(place, 1), :]
            for i in range(7):
                total = total + zr[i, taps, pl.ds(place, 1), :]
            for k in range(TAPS):
                fs[row, group * TAPS + k : group * TAPS + k + 1, :] = total[k]
    final = [
        send(fs.at[1], fr.at[0], f_s.at[0], f_r.at[0], twin),
        send(fs.at[0], fr.at[1], f_s.at[1], f_r.at[1], mirror_a),
        send(fs.at[1], fr.at[2], f_s.at[2], f_r.at[2], mirror_b),
    ]

    total = jnp.zeros((1024, 256), F32)
    for k in range(K):
        total = total + dot(rk[k, :, 0:256], wb_own[k].reshape(256, 256), 1, 1)
    acc[...] = total

    for copy in d_gather:
        copy.wait_recv()

    def other_weight(k):
        return jnp.concatenate([wb_oth[k, b, a] for a in range(4) for b in range(4)], axis=0)

    total = acc[...]
    for k in range(K):
        total = total + dot(rk[k, :, 256:512], other_weight(k), 1, 1)
    acc[...] = total
    for seq in range(2):
        eo[:, 0:256] = acc[seq * 256 : seq * 256 + 256, :].astype(BF16)
        eo[:, 256:512] = acc[512 + seq * 256 : 768 + seq * 256, :].astype(BF16)
        gi[seq] = dot(eo[...], sv[...], 1, 0).astype(BF16)

    drain()
    for copy in final:
        copy.wait_recv()
    gw[:, 0, own_lanes] = fs[0, 0:K, :]
    gw[:, 0, oth_lanes] = fr[0, 0:K, :]
    value = fr[1:3].reshape(32, 256)
    high = value.astype(BF16)
    rest = value - high.astype(F32)
    mid = rest.astype(BF16)
    low = (rest - mid.astype(F32)).astype(BF16)
    reverse = dot(jnp.concatenate([high, mid, low], axis=0), flip, 1, 0)
    reverse = reverse[0:32] + reverse[32:64] + reverse[64:96]
    for half, lanes in enumerate((own_lanes, oth_lanes)):
        for k in range(K):
            gw[k, 1:2, lanes] = reverse[half * 16 + 8 - k : half * 16 + 9 - k]
    for side, at_end in enumerate((last_pos, first_pos)):

        @pl.when(jnp.logical_not(at_end))
        def _(side=side):
            edges[2 * side].wait_send()
            edges[2 * side + 1].wait_send()


def on_device(inputs, pre_act, grad_out, weight):
    sorts = jnp.asarray(channel_orders())
    dma = pltpu.SemaphoreType.DMA
    vmem = pltpu.VMEM
    grad_input, grad_weight = pl.pallas_call(
        kernel,
        out_shape=(vmem((2, 256, 512), BF16), vmem((K, 2, 512), F32)),
        in_specs=[pl.BlockSpec(memory_space=pl.ANY)] * 5,
        out_specs=[pl.BlockSpec(memory_space=vmem)] * 2,
        scratch_shapes=[
            vmem((K, 2, 512), BF16),
            vmem((2, 2, 256, 256), BF16),
            vmem((2, 2, 256, 256), BF16),
            vmem((2, 256, 512), BF16),
            vmem((512, 512), BF16),
            vmem((2, 256 + 2 * HALO, 512), F32),
            vmem((2, 256 + 2 * HALO, 512), F32),
            vmem((256, 1024), BF16),
            vmem((2, 256, 64), BF16),
            vmem((2, 16, 512), BF16),
            vmem((2, 16, 512), BF16),
            vmem((K, 1024, 512), BF16),
            vmem((2, 2 * HALO, 512), BF16),
            vmem((4, 2 * HALO, 512), BF16),
            vmem((4, 4, 2 * HALO, 256), F32),
            vmem((K, 64, 256), BF16),
            vmem((3, 16, 256), BF16),
            vmem((3, 16, 256), BF16),
            vmem((K, 16, 256), F32),
            vmem((K, 4, 4, 16, 256), BF16),
            vmem((K, 4, 4, 16, 256), BF16),
            vmem((K, 4, 4, 16, 256), F32),
            vmem((K, 4, 4, 16, 256), BF16),
            vmem((K, 4, 4, 16, 256), BF16),
            vmem((K, 4, 4, 16, 256), BF16),
            vmem((3, K, 4, 16, 256), BF16),
            vmem((K, 4, 16, 256), F32),
            vmem((K, 4, 16, 256), BF16),
            vmem((3, K, 16, 256), BF16),
            vmem((K, 16, 256), F32),
            vmem((7, K, 16, 256), F32),
            vmem((2, 16, 256), F32),
            vmem((3, 16, 256), F32),
            vmem((1024, 256), F32),
            vmem((256, 512), BF16),
            dma((7,)),
            dma((3,)), dma((3,)), dma((4,)), dma((4,)), dma((1,)), dma((1,)), dma((7,)), dma((7,)),
            dma((3,)), dma((3,)), dma((3,)), dma((3,)), dma((4,)), dma((4,)),
            dma((GROUPS,)), dma((GROUPS,)), dma((GROUPS, 3)), dma((GROUPS, 3)),
            dma((GROUPS, 3)), dma((GROUPS, 3)), dma((GROUPS, 7)), dma((GROUPS, 7)), dma((3,)), dma((3,)),
        ],
        compiler_params=pltpu.CompilerParams(
            collective_id=0, has_side_effects=True, vmem_limit_bytes=56 << 20
        ),
        name="conv_backward",
    )(jnp.transpose(weight, (1, 0, 2)), pre_act, grad_out, inputs, sorts)
    return grad_input, jnp.transpose(grad_weight, (1, 0, 2))


def solution(mesh):
    placed = (
        P("dp", "pos", None),
        P("dp", "pos", None),
        P("dp", "pos", None),
        P(("dp", "pos"), None, None),
    )
    return jax.shard_map(
        on_device,
        mesh=mesh,
        in_specs=placed,
        out_specs=(P("dp", "pos", None), P(("dp", "pos"), None, None)),
        check_vma=False,
    )
```

```python
import jax
import jax.numpy as jnp
import numpy as np
from jax import lax
from jax.experimental import pallas as pl
from jax.experimental.pallas import tpu as pltpu
from jax.sharding import PartitionSpec as P

K = 9
HALO = 8
GROUPS = 3
TAPS = K // GROUPS
MESH = pl.DeviceIdType.MESH
F32 = jnp.float32
BF16 = jnp.bfloat16


def gelu_slope(values):
    cdf = 0.5 * (1.0 + lax.erf(values * 0.7071067811865476))
    return cdf + values * jnp.exp(-0.5 * values * values) * 0.3989422804014327


def device(x, y, z, c):
    return ((y * 4 + z % 4) * 2 + c, (z // 4) * 4 + x)


def channel_orders():
    sorts = np.zeros((2, 512, 512), np.float32)
    for core in range(2):
        for q in range(4):
            for p in range(4):
                x, y = (p, q) if core == 0 else (q, p)
                for z in range(8):
                    for c in range(2):
                        row = (q * 4 + p) * 16 + 2 * z + c
                        dp, pos = device(x, y, z, c)
                        even = 2 * (dp * 8 + pos)
                        sorts[core, row, even] = 1.0
                        sorts[core, 256 + row, 511 - even] = 1.0
    return sorts.astype(jnp.bfloat16)


def dot(a, b, ca, cb):
    return lax.dot_general(a, b, (((ca,), (cb,)), ((), ())), preferred_element_type=F32)


def kernel(
    w_hbm, pre_hbm, go_hbm, x_hbm, sort_hbm, gi, gw,
    w_ref, pv, gv, xv, sv, gp, gfp, xt, xe, x_out, x_in, rk, edge_out, edge_in, edge_pad, edge_rows,
    mirror_out, mirror_in, zb, wb_own, wb_oth,
    sf, sd, dr, qs, qr, t1, ps, pr, zs, zr, fs, fr, acc, eo,
    load_sem, m_s, m_r, h_s, h_r, x_s, x_r, z_s, z_r, p_s, p_r, q_s, q_r, d_s, d_r,
    rd_s, rd_r, rq_s, rq_r, rp_s, rp_r, rz_s, rz_r, f_s, f_r,
):
    dp, pos = lax.axis_index("dp"), lax.axis_index("pos")
    y, c = dp // 8, dp % 2
    x = pos % 4
    z = (pos // 4) * 4 + (dp // 2) % 4
    p = x * (1 - c) + y * c
    q = y * (1 - c) + x * c
    z_steps = (4, 3, 5, 2, 6, 1, 7)
    z_peers = [device(x, y, (z + i) % 8, c) for i in z_steps]
    p_peers = [device((x + i * (1 - c)) % 4, (y + i * c) % 4, z, c) for i in range(1, 4)]
    q_peers = [device((x + i * c) % 4, (y + i * (1 - c)) % 4, z, c) for i in range(1, 4)]
    twin = device(x, y, z, 1 - c)
    mirror_a = device(3 - x, 3 - y, 7 - z, 1 - c)
    mirror_b = device(3 - x, 3 - y, 7 - z, c)
    other = dp + 1 - 2 * c
    beside = [(row, place) for place in ((pos + 1) % 8, (pos + 7) % 8) for row in (dp, other)]

    barrier = pltpu.get_barrier_semaphore()
    peers = [mirror_a, mirror_b] + beside + z_peers + p_peers + q_peers + [twin]
    for peer in peers:
        pl.semaphore_signal(barrier, inc=1, device_id=peer, device_id_type=MESH)

    own_lanes = pl.ds(pl.multiple_of(c * 256, 256), 256)
    oth_lanes = pl.ds(pl.multiple_of((1 - c) * 256, 256), 256)
    loads = [
        pltpu.make_async_copy(pre_hbm.at[:, :, own_lanes], pv.at[0], load_sem.at[0]),
        pltpu.make_async_copy(go_hbm.at[:, :, own_lanes], gv.at[0], load_sem.at[1]),
        pltpu.make_async_copy(pre_hbm.at[:, :, oth_lanes], pv.at[1], load_sem.at[2]),
        pltpu.make_async_copy(go_hbm.at[:, :, oth_lanes], gv.at[1], load_sem.at[3]),
        pltpu.make_async_copy(x_hbm, xv, load_sem.at[4]),
        pltpu.make_async_copy(sort_hbm.at[c], sv, load_sem.at[5]),
        pltpu.make_async_copy(w_hbm, w_ref, load_sem.at[6]),
    ]
    for load in loads:
        load.start()

    sends = []

    def drain():
        while sends:
            sends.pop(0).wait_send()


    def send(src, dst, send_sem, recv_sem, peer):
        copy = pltpu.make_async_remote_copy(
            src_ref=src, dst_ref=dst, send_sem=send_sem, recv_sem=recv_sem,
            device_id=peer, device_id_type=MESH,
        )
        copy.start()
        sends.append(copy)
        return copy

    rows_i = lax.broadcasted_iota(jnp.int32, (256, 256), 0)
    cols_i = lax.broadcasted_iota(jnp.int32, (256, 256), 1)
    flip = jnp.where(rows_i + cols_i == 255, 1.0, 0.0).astype(BF16)

    zeros = jnp.zeros((2, HALO, 512), F32)
    for padded in (gp, gfp):
        padded[:, 0:HALO, :] = zeros
        padded[:, HALO + 256 : 2 * HALO + 256, :] = zeros
    for half in range(2):
        loads[2 * half].wait()
        loads[2 * half + 1].wait()
        for seq in range(2):

            def slope(i, carry, half=half, seq=seq):
                rows = pl.ds(pl.multiple_of(i * 32, 32), 32)
                values = pv[half, seq, rows, :].astype(F32)
                grad = gv[half, seq, rows, :].astype(F32) * gelu_slope(values)
                place = pl.ds(pl.multiple_of(HALO + i * 32, 8), 32)
                gp[seq, place, half * 256 : half * 256 + 256] = grad.astype(BF16).astype(F32)
                return carry

            lax.fori_loop(0, 8, slope, 0)
    loads[6].wait()
    w_own = w_ref[:, :, own_lanes].astype(F32)
    w_oth = w_ref[:, :, oth_lanes].astype(F32)
    w0_own = w_own[:, 0, :]
    for i, row in enumerate((w_own[:, 1, :], w_oth[:, 1, :], w_oth[:, 0, :])):
        mirror_out[i] = jnp.concatenate([row, jnp.zeros((16 - K, 256), F32)], axis=0).astype(BF16)

    edge_out[0] = gp[:, 256 : 256 + HALO, :].reshape(2 * HALO, 512).astype(BF16)
    edge_out[1] = gp[:, HALO : 2 * HALO, :].reshape(2 * HALO, 512).astype(BF16)

    loads[4].wait()
    for end, start in enumerate((0, 248)):
        ends = [xv[seq, start : start + 8, :].astype(F32) for seq in range(2)]
        x_out[end] = jnp.concatenate(ends, axis=0).astype(BF16)

    pl.semaphore_wait(barrier, len(peers))
    mirror = [
        send(mirror_out.at[i], mirror_in.at[i], m_s.at[i], m_r.at[i], peer)
        for i, peer in enumerate((mirror_a, mirror_b, twin))
    ]
    edges = [
        pltpu.make_async_remote_copy(
            src_ref=edge_out.at[i // 2], dst_ref=edge_in.at[i],
            send_sem=h_s.at[i], recv_sem=h_r.at[i],
            device_id=peer, device_id_type=MESH,
        )
        for i, peer in enumerate(beside)
    ]
    last_pos, first_pos = pos == 7, pos == 0
    for side, at_end in enumerate((last_pos, first_pos)):

        @pl.when(jnp.logical_not(at_end))
        def _(side=side):
            edges[2 * side].start()
            edges[2 * side + 1].start()

    x_ends = send(x_out, x_in, x_s.at[0], x_r.at[0], twin)

    for seq in range(2):
        main = gp[seq, HALO : HALO + 256, :].astype(BF16)
        gfp[seq, HALO : HALO + 256, 0:256] = dot(main[:, 256:512], flip, 1, 0)
        gfp[seq, HALO : HALO + 256, 256:512] = dot(main[:, 0:256], flip, 1, 0)
    loads[5].wait()
    for seq in range(2):
        sorted_x = dot(sv[...], xv[seq], 1, 1).astype(BF16)
        xt[:, seq * 256 : seq * 256 + 256] = sorted_x[0:256]
        xt[:, 512 + seq * 256 : 768 + seq * 256] = sorted_x[256:512]
    for k in range(K):
        for seq in range(2):
            rk[k, seq * 256 : seq * 256 + 256, :] = gp[seq, 12 - k : 268 - k, :].astype(BF16)
            rk[k, 512 + seq * 256 : 768 + seq * 256, :] = gfp[seq, 4 + k : 260 + k, :].astype(BF16)

    def inner(k, carry):
        terms = dot(xt[...], rk[k], 1, 0)
        sf[k] = terms[:, 0:256].reshape(4, 4, 16, 256)
        for a in range(4):
            for b in range(4):
                rows = slice((a * 4 + b) * 16, (a * 4 + b) * 16 + 16)
                sd[k, b, a] = terms[rows, 256:512].astype(BF16)
        return carry

    twin_copies = []
    for group in range(GROUPS):
        lax.fori_loop(group * TAPS, group * TAPS + TAPS, inner, 0, unroll=True)
        taps = pl.ds(group * TAPS, TAPS)
        twin_copies.append(send(sd.at[taps], dr.at[taps], rd_s.at[group], rd_r.at[group], twin))

    x_ends.wait_recv()
    blank = jnp.zeros((32, 512), BF16)
    for i in range(2):
        even_rows = jnp.concatenate([x_out[1 - i], x_in[1 - i], blank], axis=0)
        odd_rows = jnp.concatenate([blank, x_out[i], x_in[i]], axis=0)
        xe[i] = (dot(sv[0:256, :], even_rows, 1, 1) + dot(sv[256:512, :], odd_rows, 1, 1)).astype(BF16)
    for copy in mirror:
        copy.wait_recv()
    rev_a = dot(mirror_in[0], flip, 1, 0)
    rev_b = dot(mirror_in[1], flip, 1, 0)
    w0_oth = mirror_in[2].astype(F32)
    for k in range(K):
        zb[k, pl.ds(2 * z + c, 1), :] = w0_own[k : k + 1] + rev_a[8 - k : 9 - k]
        zb[k, pl.ds(2 * z + 1 - c, 1), :] = w0_oth[k : k + 1] + rev_b[8 - k : 9 - k]
    mine = pl.ds(2 * z, 2)
    z_gather = [
        send(zb.at[:, mine, :], zb.at[:, mine, :], z_s.at[i], z_r.at[i], peer)
        for i, peer in enumerate(z_peers)
    ]

    for side, at_end in enumerate((first_pos, last_pos)):

        @pl.when(jnp.logical_not(at_end))
        def _(side=side):
            edges[2 * side].wait_recv()
            edges[2 * side + 1].wait_recv()

    border = [
        [jnp.where(at_end, 0.0, edge_in[2 * side + core].astype(F32)) for core in range(2)]
        for side, at_end in enumerate((first_pos, last_pos))
    ]
    low, high = [
        [
            border[side][core][seq * HALO : seq * HALO + HALO, core * 256 : core * 256 + 256]
            for core in range(2)
            for seq in range(2)
        ]
        for side in range(2)
    ]
    reverse_of = jnp.concatenate(
        [
            border[side][core][:, 256 - core * 256 : 512 - core * 256]
            for side in range(2)
            for core in range(2)
        ],
        axis=0,
    ).astype(BF16)
    reverse_of = dot(reverse_of, flip, 1, 0)
    blank = jnp.zeros((HALO, 256), F32)
    for seq in range(4):
        rev_low = reverse_of[seq * HALO : seq * HALO + HALO]
        rev_high = reverse_of[(4 + seq) * HALO : (5 + seq) * HALO]
        for i, parts in enumerate(
            ((blank, high[seq]), (rev_low, blank), (low[seq], blank), (blank, rev_high))
        ):
            edge_pad[i, seq, 0:HALO, :] = parts[0]
            edge_pad[i, seq, HALO : 2 * HALO, :] = parts[1]
    for k in range(K):
        first, second = (0, 1) if k <= 4 else (2, 3)
        start_1, start_2 = (4 - k, 4 + k) if k <= 4 else (12 - k, k - 4)
        rows_1 = [edge_pad[first, seq, start_1 : start_1 + 8, :] for seq in range(4)]
        rows_2 = [edge_pad[second, seq, start_2 : start_2 + 8, :] for seq in range(4)]
        edge_rows[k] = jnp.concatenate(rows_1 + rows_2, axis=0).astype(BF16)

    def chip_sum(group):
        twin_copies[group].wait_recv()

        def one(k, carry):
            terms = dot(xe[k // 5], edge_rows[k], 1, 0).reshape(4, 4, 16, 256)
            total = sf[k] + dr[k].astype(F32) + terms
            sf[k] = total
            qs[k] = total.astype(BF16)
            return carry

        lax.fori_loop(group * TAPS, group * TAPS + TAPS, one, 0, unroll=True)
        taps = pl.ds(group * TAPS, TAPS)
        return [
            send(
                qs.at[taps, (q + i) % 4], qr.at[i - 1, taps],
                rq_s.at[group, i - 1], rq_r.at[group, i - 1], q_peers[i - 1],
            )
            for i in (2, 1, 3)
        ]

    def q_sum(group, copies):
        for copy in copies:
            copy.wait_recv()

        def one(k, carry):
            total = sf[k, q] + qr[0, k].astype(F32) + qr[1, k].astype(F32) + qr[2, k].astype(F32)
            t1[k] = total
            ps[k] = total.astype(BF16)
            return carry

        lax.fori_loop(group * TAPS, group * TAPS + TAPS, one, 0, unroll=True)
        taps = pl.ds(group * TAPS, TAPS)
        return [
            send(
                ps.at[taps, (p + i) % 4], pr.at[i - 1, taps],
                rp_s.at[group, i - 1], rp_r.at[group, i - 1], p_peers[i - 1],
            )
            for i in (2, 1, 3)
        ]

    q_copies = [chip_sum(group) for group in range(GROUPS)]

    low = jnp.where(first_pos, 0.0, edge_in[0].astype(F32)).reshape(2, HALO, 512)
    high = jnp.where(last_pos, 0.0, edge_in[2].astype(F32)).reshape(2, HALO, 512)
    gp[:, 0:HALO, :] = low
    gp[:, HALO + 256 : 2 * HALO + 256, :] = high
    both = jnp.concatenate([low[0], low[1], high[0], high[1]], axis=0).astype(BF16)
    both = jnp.concatenate(
        [dot(both[:, 256:512], flip, 1, 0), dot(both[:, 0:256], flip, 1, 0)], axis=1
    )
    for seq in range(2):
        gfp[seq, 0:HALO, :] = both[seq * HALO : seq * HALO + HALO]
        gfp[seq, HALO + 256 : 2 * HALO + 256, :] = both[(2 + seq) * HALO : (3 + seq) * HALO]
    for k in range(K):
        for seq in range(2):
            for start in (0, 240):
                rk[k, seq * 256 + start : seq * 256 + start + 16, :] = gp[
                    seq, 12 - k + start : 28 - k + start, :
                ].astype(BF16)
                rk[k, 512 + seq * 256 + start : 528 + seq * 256 + start, :] = gfp[
                    seq, 4 + k + start : 20 + k + start, :
                ].astype(BF16)

    for copy in z_gather:
        copy.wait_recv()
    wb_own[:, q, p] = zb[...].astype(BF16)
    p_gather = [
        send(wb_own.at[:, q, p], wb_own.at[:, q, p], p_s.at[i], p_r.at[i], peer)
        for i, peer in enumerate(p_peers)
    ]
    p_copies = [q_sum(group, q_copies[group]) for group in range(GROUPS)]
    for copy in p_gather:
        copy.wait_recv()
    q_gather = [
        send(wb_own.at[:, q], wb_own.at[:, q], q_s.at[i], q_r.at[i], peer)
        for i, peer in enumerate(q_peers)
    ]
    d_gather = [send(wb_own.at[:, q], wb_oth.at[:, q], d_s.at[0], d_r.at[0], twin)]
    def p_sum(k, carry):
        zs[k] = t1[k, p] + pr[0, k].astype(F32) + pr[1, k].astype(F32) + pr[2, k].astype(F32)
        return carry

    z_scatter = []
    for group in range(GROUPS):
        for copy in p_copies[group]:
            copy.wait_recv()
        lax.fori_loop(group * TAPS, group * TAPS + TAPS, p_sum, 0, unroll=True)
        taps = pl.ds(group * TAPS, TAPS)
        for i, step in enumerate(z_steps):
            rows = pl.ds(2 * ((z + step) % 8), 2)
            z_scatter.append(
                send(
                    zs.at[taps, rows, :], zr.at[i, taps, rows, :],
                    rz_s.at[group, i], rz_r.at[group, i], z_peers[i],
                )
            )

    for i in range(1, 4):
        q_gather[i - 1].wait_recv()
        from_q = (q + 4 - i) % 4
        d_gather.append(
            send(wb_own.at[:, from_q], wb_oth.at[:, from_q], d_s.at[i], d_r.at[i], twin)
        )

    fs[:, 8:16, :] = jnp.zeros((2, 8, 256), F32)
    for group in range(GROUPS):
        for copy in z_scatter[group * 7 : group * 7 + 7]:
            copy.wait_recv()
        taps = slice(group * TAPS, group * TAPS + TAPS)
        for row, place in enumerate((2 * z + c, 2 * z + 1 - c)):
            total = zs[taps, pl.ds(place, 1), :]
            for i in range(7):
                total = total + zr[i, taps, pl.ds(place, 1), :]
            for k in range(TAPS):
                fs[row, group * TAPS + k : group * TAPS + k + 1, :] = total[k]
    final = [
        send(fs.at[1], fr.at[0], f_s.at[0], f_r.at[0], twin),
        send(fs.at[0], fr.at[1], f_s.at[1], f_r.at[1], mirror_a),
        send(fs.at[1], fr.at[2], f_s.at[2], f_r.at[2], mirror_b),
    ]

    total = jnp.zeros((1024, 256), F32)
    for k in range(K):
        total = total + dot(rk[k, :, 0:256], wb_own[k].reshape(256, 256), 1, 1)
    acc[...] = total

    for copy in d_gather:
        copy.wait_recv()

    def other_weight(k):
        return jnp.concatenate([wb_oth[k, b, a] for a in range(4) for b in range(4)], axis=0)

    total = acc[...]
    for k in range(K):
        total = total + dot(rk[k, :, 256:512], other_weight(k), 1, 1)
    acc[...] = total
    for seq in range(2):
        eo[:, 0:256] = acc[seq * 256 : seq * 256 + 256, :].astype(BF16)
        eo[:, 256:512] = acc[512 + seq * 256 : 768 + seq * 256, :].astype(BF16)
        gi[seq] = dot(eo[...], sv[...], 1, 0).astype(BF16)

    drain()
    for copy in final:
        copy.wait_recv()
    gw[:, 0, own_lanes] = fs[0, 0:K, :]
    gw[:, 0, oth_lanes] = fr[0, 0:K, :]
    value = fr[1:3].reshape(32, 256)
    high = value.astype(BF16)
    rest = value - high.astype(F32)
    mid = rest.astype(BF16)
    low = (rest - mid.astype(F32)).astype(BF16)
    reverse = dot(jnp.concatenate([high, mid, low], axis=0), flip, 1, 0)
    reverse = reverse[0:32] + reverse[32:64] + reverse[64:96]
    for half, lanes in enumerate((own_lanes, oth_lanes)):
        for k in range(K):
            gw[k, 1:2, lanes] = reverse[half * 16 + 8 - k : half * 16 + 9 - k]
    for side, at_end in enumerate((last_pos, first_pos)):

        @pl.when(jnp.logical_not(at_end))
        def _(side=side):
            edges[2 * side].wait_send()
            edges[2 * side + 1].wait_send()


def on_device(inputs, pre_act, grad_out, weight):
    sorts = jnp.asarray(channel_orders())
    dma = pltpu.SemaphoreType.DMA
    vmem = pltpu.VMEM
    grad_input, grad_weight = pl.pallas_call(
        kernel,
        out_shape=(vmem((2, 256, 512), BF16), vmem((K, 2, 512), F32)),
        in_specs=[pl.BlockSpec(memory_space=pl.ANY)] * 5,
        out_specs=[pl.BlockSpec(memory_space=vmem)] * 2,
        scratch_shapes=[
            vmem((K, 2, 512), BF16),
            vmem((2, 2, 256, 256), BF16),
            vmem((2, 2, 256, 256), BF16),
            vmem((2, 256, 512), BF16),
            vmem((512, 512), BF16),
            vmem((2, 256 + 2 * HALO, 512), F32),
            vmem((2, 256 + 2 * HALO, 512), F32),
            vmem((256, 1024), BF16),
            vmem((2, 256, 64), BF16),
            vmem((2, 16, 512), BF16),
            vmem((2, 16, 512), BF16),
            vmem((K, 1024, 512), BF16),
            vmem((2, 2 * HALO, 512), BF16),
            vmem((4, 2 * HALO, 512), BF16),
            vmem((4, 4, 2 * HALO, 256), F32),
            vmem((K, 64, 256), BF16),
            vmem((3, 16, 256), BF16),
            vmem((3, 16, 256), BF16),
            vmem((K, 16, 256), F32),
            vmem((K, 4, 4, 16, 256), BF16),
            vmem((K, 4, 4, 16, 256), BF16),
            vmem((K, 4, 4, 16, 256), F32),
            vmem((K, 4, 4, 16, 256), BF16),
            vmem((K, 4, 4, 16, 256), BF16),
            vmem((K, 4, 4, 16, 256), BF16),
            vmem((3, K, 4, 16, 256), BF16),
            vmem((K, 4, 16, 256), F32),
            vmem((K, 4, 16, 256), BF16),
            vmem((3, K, 16, 256), BF16),
            vmem((K, 16, 256), F32),
            vmem((7, K, 16, 256), F32),
            vmem((2, 16, 256), F32),
            vmem((3, 16, 256), F32),
            vmem((1024, 256), F32),
            vmem((256, 512), BF16),
            dma((7,)),
            dma((3,)), dma((3,)), dma((4,)), dma((4,)), dma((1,)), dma((1,)), dma((7,)), dma((7,)),
            dma((3,)), dma((3,)), dma((3,)), dma((3,)), dma((4,)), dma((4,)),
            dma((GROUPS,)), dma((GROUPS,)), dma((GROUPS, 3)), dma((GROUPS, 3)),
            dma((GROUPS, 3)), dma((GROUPS, 3)), dma((GROUPS, 7)), dma((GROUPS, 7)), dma((3,)), dma((3,)),
        ],
        compiler_params=pltpu.CompilerParams(
            collective_id=0, has_side_effects=True, vmem_limit_bytes=56 << 20
        ),
        name="conv_backward",
    )(jnp.transpose(weight, (1, 0, 2)), pre_act, grad_out, inputs, sorts)
    return grad_input, jnp.transpose(grad_weight, (1, 0, 2))


def solution(mesh):
    placed = (
        P("dp", "pos", None),
        P("dp", "pos", None),
        P("dp", "pos", None),
        P(("dp", "pos"), None, None),
    )
    return jax.shard_map(
        on_device,
        mesh=mesh,
        in_specs=placed,
        out_specs=(P("dp", "pos", None), P(("dp", "pos"), None, None)),
        check_vma=False,
    )
```

```python
import jax
import jax.numpy as jnp
import numpy as np
from jax import lax
from jax.experimental import pallas as pl
from jax.experimental.pallas import tpu as pltpu
from jax.sharding import PartitionSpec as P

K = 9
HALO = 8
GROUPS = 3
TAPS = K // GROUPS
MESH = pl.DeviceIdType.MESH
F32 = jnp.float32
BF16 = jnp.bfloat16


def gelu_slope(values):
    cdf = 0.5 * (1.0 + lax.erf(values * 0.7071067811865476))
    return cdf + values * jnp.exp(-0.5 * values * values) * 0.3989422804014327


def device(x, y, z, c):
    return ((y * 4 + z % 4) * 2 + c, (z // 4) * 4 + x)


def channel_orders():
    sorts = np.zeros((2, 512, 512), np.float32)
    for core in range(2):
        for q in range(4):
            for p in range(4):
                x, y = (p, q) if core == 0 else (q, p)
                for z in range(8):
                    for c in range(2):
                        row = (q * 4 + p) * 16 + 2 * z + c
                        dp, pos = device(x, y, z, c)
                        even = 2 * (dp * 8 + pos)
                        sorts[core, row, even] = 1.0
                        sorts[core, 256 + row, 511 - even] = 1.0
    return sorts.astype(jnp.bfloat16)


def dot(a, b, ca, cb):
    return lax.dot_general(a, b, (((ca,), (cb,)), ((), ())), preferred_element_type=F32)


def kernel(
    w_hbm, pre_hbm, go_hbm, x_hbm, sort_hbm, gi, gw,
    w_ref, pv, gv, xv, sv, gp, gfp, xt, xe, x_out, x_in, rk, edge_out, edge_in, edge_pad, edge_rows,
    mirror_out, mirror_in, zb, wb_own, wb_oth,
    sf, sd, dr, qs, qr, t1, ps, pr, zs, zr, fs, fr, acc, eo,
    load_sem, m_s, m_r, h_s, h_r, x_s, x_r, z_s, z_r, p_s, p_r, q_s, q_r, d_s, d_r,
    rd_s, rd_r, rq_s, rq_r, rp_s, rp_r, rz_s, rz_r, f_s, f_r,
):
    dp, pos = lax.axis_index("dp"), lax.axis_index("pos")
    y, c = dp // 8, dp % 2
    x = pos % 4
    z = (pos // 4) * 4 + (dp // 2) % 4
    p = x * (1 - c) + y * c
    q = y * (1 - c) + x * c
    z_steps = (4, 3, 5, 2, 6, 1, 7)
    z_peers = [device(x, y, (z + i) % 8, c) for i in z_steps]
    p_steps = (2, 1, 3)
    p_peers = [device((x + i * (1 - c)) % 4, (y + i * c) % 4, z, c) for i in p_steps]
    q_peers = [device((x + i * c) % 4, (y + i * (1 - c)) % 4, z, c) for i in p_steps]
    twin = device(x, y, z, 1 - c)
    mirror_a = device(3 - x, 3 - y, 7 - z, 1 - c)
    mirror_b = device(3 - x, 3 - y, 7 - z, c)
    other = dp + 1 - 2 * c
    beside = [(row, place) for place in ((pos + 1) % 8, (pos + 7) % 8) for row in (dp, other)]

    barrier = pltpu.get_barrier_semaphore()
    peers = [mirror_a, mirror_b] + beside + z_peers + p_peers + q_peers + [twin]
    for peer in peers:
        pl.semaphore_signal(barrier, inc=1, device_id=peer, device_id_type=MESH)

    own_lanes = pl.ds(pl.multiple_of(c * 256, 256), 256)
    oth_lanes = pl.ds(pl.multiple_of((1 - c) * 256, 256), 256)
    loads = [
        pltpu.make_async_copy(pre_hbm.at[:, :, own_lanes], pv.at[0], load_sem.at[0]),
        pltpu.make_async_copy(go_hbm.at[:, :, own_lanes], gv.at[0], load_sem.at[1]),
        pltpu.make_async_copy(pre_hbm.at[:, :, oth_lanes], pv.at[1], load_sem.at[2]),
        pltpu.make_async_copy(go_hbm.at[:, :, oth_lanes], gv.at[1], load_sem.at[3]),
        pltpu.make_async_copy(x_hbm, xv, load_sem.at[4]),
        pltpu.make_async_copy(sort_hbm.at[c], sv, load_sem.at[5]),
        pltpu.make_async_copy(w_hbm, w_ref, load_sem.at[6]),
    ]
    for load in loads:
        load.start()

    sends = []

    def drain():
        while sends:
            sends.pop(0).wait_send()


    def send(src, dst, send_sem, recv_sem, peer):
        copy = pltpu.make_async_remote_copy(
            src_ref=src, dst_ref=dst, send_sem=send_sem, recv_sem=recv_sem,
            device_id=peer, device_id_type=MESH,
        )
        copy.start()
        sends.append(copy)
        return copy

    rows_i = lax.broadcasted_iota(jnp.int32, (256, 256), 0)
    cols_i = lax.broadcasted_iota(jnp.int32, (256, 256), 1)
    flip = jnp.where(rows_i + cols_i == 255, 1.0, 0.0).astype(BF16)

    zeros = jnp.zeros((2, HALO, 512), F32)
    for padded in (gp, gfp):
        padded[:, 0:HALO, :] = zeros
        padded[:, HALO + 256 : 2 * HALO + 256, :] = zeros
    for half in range(2):
        loads[2 * half].wait()
        loads[2 * half + 1].wait()
        for seq in range(2):

            def slope(i, carry, half=half, seq=seq):
                rows = pl.ds(pl.multiple_of(i * 32, 32), 32)
                values = pv[half, seq, rows, :].astype(F32)
                grad = gv[half, seq, rows, :].astype(F32) * gelu_slope(values)
                place = pl.ds(pl.multiple_of(HALO + i * 32, 8), 32)
                gp[seq, place, half * 256 : half * 256 + 256] = grad.astype(BF16).astype(F32)
                return carry

            lax.fori_loop(0, 8, slope, 0)
    loads[6].wait()
    w_own = w_ref[:, :, own_lanes].astype(F32)
    w_oth = w_ref[:, :, oth_lanes].astype(F32)
    w0_own = w_own[:, 0, :]
    for i, row in enumerate((w_own[:, 1, :], w_oth[:, 1, :], w_oth[:, 0, :])):
        mirror_out[i] = jnp.concatenate([row, jnp.zeros((16 - K, 256), F32)], axis=0).astype(BF16)

    edge_out[0] = gp[:, 256 : 256 + HALO, :].reshape(2 * HALO, 512).astype(BF16)
    edge_out[1] = gp[:, HALO : 2 * HALO, :].reshape(2 * HALO, 512).astype(BF16)

    loads[4].wait()
    for end, start in enumerate((0, 248)):
        ends = [xv[seq, start : start + 8, :].astype(F32) for seq in range(2)]
        x_out[end] = jnp.concatenate(ends, axis=0).astype(BF16)

    pl.semaphore_wait(barrier, len(peers))
    edges = [
        pltpu.make_async_remote_copy(
            src_ref=edge_out.at[i // 2], dst_ref=edge_in.at[i],
            send_sem=h_s.at[i], recv_sem=h_r.at[i],
            device_id=peer, device_id_type=MESH,
        )
        for i, peer in enumerate(beside)
    ]
    last_pos, first_pos = pos == 7, pos == 0
    for side, at_end in enumerate((last_pos, first_pos)):

        @pl.when(jnp.logical_not(at_end))
        def _(side=side):
            edges[2 * side].start()
            edges[2 * side + 1].start()

    mirror = [
        send(mirror_out.at[i], mirror_in.at[i], m_s.at[i], m_r.at[i], peer)
        for i, peer in enumerate((mirror_a, mirror_b, twin))
    ]
    x_ends = send(x_out, x_in, x_s.at[0], x_r.at[0], twin)

    for seq in range(2):
        main = gp[seq, HALO : HALO + 256, :].astype(BF16)
        gfp[seq, HALO : HALO + 256, 0:256] = dot(main[:, 256:512], flip, 1, 0)
        gfp[seq, HALO : HALO + 256, 256:512] = dot(main[:, 0:256], flip, 1, 0)
    loads[5].wait()
    for seq in range(2):
        sorted_x = dot(sv[...], xv[seq], 1, 1).astype(BF16)
        xt[:, seq * 256 : seq * 256 + 256] = sorted_x[0:256]
        xt[:, 512 + seq * 256 : 768 + seq * 256] = sorted_x[256:512]
    for k in range(K):
        for seq in range(2):
            rk[k, seq * 256 : seq * 256 + 256, :] = gp[seq, 12 - k : 268 - k, :].astype(BF16)
            rk[k, 512 + seq * 256 : 768 + seq * 256, :] = gfp[seq, 4 + k : 260 + k, :].astype(BF16)

    def inner(k, carry):
        terms = dot(xt[...], rk[k], 1, 0)
        sf[k] = terms[:, 0:256].reshape(4, 4, 16, 256)
        for a in range(4):
            for b in range(4):
                rows = slice((a * 4 + b) * 16, (a * 4 + b) * 16 + 16)
                sd[k, b, a] = terms[rows, 256:512].astype(BF16)
        return carry

    twin_copies = []
    for group in range(GROUPS):
        lax.fori_loop(group * TAPS, group * TAPS + TAPS, inner, 0, unroll=True)
        taps = pl.ds(group * TAPS, TAPS)
        twin_copies.append(send(sd.at[taps], dr.at[taps], rd_s.at[group], rd_r.at[group], twin))

    x_ends.wait_recv()
    blank = jnp.zeros((32, 512), BF16)
    for i in range(2):
        even_rows = jnp.concatenate([x_out[1 - i], x_in[1 - i], blank], axis=0)
        odd_rows = jnp.concatenate([blank, x_out[i], x_in[i]], axis=0)
        xe[i] = (dot(sv[0:256, :], even_rows, 1, 1) + dot(sv[256:512, :], odd_rows, 1, 1)).astype(BF16)
    for copy in mirror:
        copy.wait_recv()
    rev_a = dot(mirror_in[0], flip, 1, 0)
    rev_b = dot(mirror_in[1], flip, 1, 0)
    w0_oth = mirror_in[2].astype(F32)
    for k in range(K):
        zb[k, pl.ds(2 * z + c, 1), :] = w0_own[k : k + 1] + rev_a[8 - k : 9 - k]
        zb[k, pl.ds(2 * z + 1 - c, 1), :] = w0_oth[k : k + 1] + rev_b[8 - k : 9 - k]
    mine = pl.ds(2 * z, 2)
    z_gather = [
        send(zb.at[:, mine, :], zb.at[:, mine, :], z_s.at[i], z_r.at[i], peer)
        for i, peer in enumerate(z_peers)
    ]

    for side, at_end in enumerate((first_pos, last_pos)):

        @pl.when(jnp.logical_not(at_end))
        def _(side=side):
            edges[2 * side].wait_recv()
            edges[2 * side + 1].wait_recv()

    border = [
        [jnp.where(at_end, 0.0, edge_in[2 * side + core].astype(F32)) for core in range(2)]
        for side, at_end in enumerate((first_pos, last_pos))
    ]
    low, high = [
        [
            border[side][core][seq * HALO : seq * HALO + HALO, core * 256 : core * 256 + 256]
            for core in range(2)
            for seq in range(2)
        ]
        for side in range(2)
    ]
    reverse_of = jnp.concatenate(
        [
            border[side][core][:, 256 - core * 256 : 512 - core * 256]
            for side in range(2)
            for core in range(2)
        ],
        axis=0,
    ).astype(BF16)
    reverse_of = dot(reverse_of, flip, 1, 0)
    blank = jnp.zeros((HALO, 256), F32)
    for seq in range(4):
        rev_low = reverse_of[seq * HALO : seq * HALO + HALO]
        rev_high = reverse_of[(4 + seq) * HALO : (5 + seq) * HALO]
        for i, parts in enumerate(
            ((blank, high[seq]), (rev_low, blank), (low[seq], blank), (blank, rev_high))
        ):
            edge_pad[i, seq, 0:HALO, :] = parts[0]
            edge_pad[i, seq, HALO : 2 * HALO, :] = parts[1]
    for k in range(K):
        first, second = (0, 1) if k <= 4 else (2, 3)
        start_1, start_2 = (4 - k, 4 + k) if k <= 4 else (12 - k, k - 4)
        rows_1 = [edge_pad[first, seq, start_1 : start_1 + 8, :] for seq in range(4)]
        rows_2 = [edge_pad[second, seq, start_2 : start_2 + 8, :] for seq in range(4)]
        edge_rows[k] = jnp.concatenate(rows_1 + rows_2, axis=0).astype(BF16)

    def chip_sum(group):
        twin_copies[group].wait_recv()

        def one(k, carry):
            terms = dot(xe[k // 5], edge_rows[k], 1, 0).reshape(4, 4, 16, 256)
            total = sf[k] + dr[k].astype(F32) + terms
            sf[k] = total
            qs[k] = total.astype(BF16)
            return carry

        lax.fori_loop(group * TAPS, group * TAPS + TAPS, one, 0, unroll=True)
        taps = pl.ds(group * TAPS, TAPS)
        return [
            send(
                qs.at[taps, (q + step) % 4], qr.at[i, taps],
                rq_s.at[group, i], rq_r.at[group, i], q_peers[i],
            )
            for i, step in enumerate(p_steps)
        ]

    def q_sum(group, copies):
        for copy in copies:
            copy.wait_recv()

        def one(k, carry):
            total = sf[k, q] + qr[0, k].astype(F32) + qr[1, k].astype(F32) + qr[2, k].astype(F32)
            t1[k] = total
            ps[k] = total.astype(BF16)
            return carry

        lax.fori_loop(group * TAPS, group * TAPS + TAPS, one, 0, unroll=True)
        taps = pl.ds(group * TAPS, TAPS)
        return [
            send(
                ps.at[taps, (p + step) % 4], pr.at[i, taps],
                rp_s.at[group, i], rp_r.at[group, i], p_peers[i],
            )
            for i, step in enumerate(p_steps)
        ]

    q_copies = [chip_sum(group) for group in range(GROUPS)]

    low = jnp.where(first_pos, 0.0, edge_in[0].astype(F32)).reshape(2, HALO, 512)
    high = jnp.where(last_pos, 0.0, edge_in[2].astype(F32)).reshape(2, HALO, 512)
    gp[:, 0:HALO, :] = low
    gp[:, HALO + 256 : 2 * HALO + 256, :] = high
    both = jnp.concatenate([low[0], low[1], high[0], high[1]], axis=0).astype(BF16)
    both = jnp.concatenate(
        [dot(both[:, 256:512], flip, 1, 0), dot(both[:, 0:256], flip, 1, 0)], axis=1
    )
    for seq in range(2):
        gfp[seq, 0:HALO, :] = both[seq * HALO : seq * HALO + HALO]
        gfp[seq, HALO + 256 : 2 * HALO + 256, :] = both[(2 + seq) * HALO : (3 + seq) * HALO]
    for k in range(K):
        for seq in range(2):
            for start in (0, 240):
                rk[k, seq * 256 + start : seq * 256 + start + 16, :] = gp[
                    seq, 12 - k + start : 28 - k + start, :
                ].astype(BF16)
                rk[k, 512 + seq * 256 + start : 528 + seq * 256 + start, :] = gfp[
                    seq, 4 + k + start : 20 + k + start, :
                ].astype(BF16)

    for copy in z_gather:
        copy.wait_recv()
    wb_own[:, q, p] = zb[...].astype(BF16)
    p_gather = [
        send(wb_own.at[:, q, p], wb_own.at[:, q, p], p_s.at[i], p_r.at[i], peer)
        for i, peer in enumerate(p_peers)
    ]
    p_copies = [q_sum(group, q_copies[group]) for group in range(GROUPS - 1)]
    for copy in p_gather:
        copy.wait_recv()
    q_gather = [
        send(wb_own.at[:, q], wb_own.at[:, q], q_s.at[i], q_r.at[i], peer)
        for i, peer in enumerate(q_peers)
    ]
    p_copies.append(q_sum(GROUPS - 1, q_copies[GROUPS - 1]))
    d_gather = [send(wb_own.at[:, q], wb_oth.at[:, q], d_s.at[0], d_r.at[0], twin)]
    def p_sum(k, carry):
        zs[k] = t1[k, p] + pr[0, k].astype(F32) + pr[1, k].astype(F32) + pr[2, k].astype(F32)
        return carry

    z_scatter = []
    for group in range(GROUPS):
        for copy in p_copies[group]:
            copy.wait_recv()
        lax.fori_loop(group * TAPS, group * TAPS + TAPS, p_sum, 0, unroll=True)
        taps = pl.ds(group * TAPS, TAPS)
        for i, step in enumerate(z_steps):
            rows = pl.ds(2 * ((z + step) % 8), 2)
            z_scatter.append(
                send(
                    zs.at[taps, rows, :], zr.at[i, taps, rows, :],
                    rz_s.at[group, i], rz_r.at[group, i], z_peers[i],
                )
            )

    for i in (1, 2, 0):
        q_gather[i].wait_recv()
        from_q = (q + 4 - p_steps[i]) % 4
        d_gather.append(
            send(wb_own.at[:, from_q], wb_oth.at[:, from_q], d_s.at[1 + i], d_r.at[1 + i], twin)
        )

    fs[:, 8:16, :] = jnp.zeros((2, 8, 256), F32)
    for group in range(GROUPS):
        for copy in z_scatter[group * 7 : group * 7 + 7]:
            copy.wait_recv()
        taps = slice(group * TAPS, group * TAPS + TAPS)
        for row, place in enumerate((2 * z + c, 2 * z + 1 - c)):
            total = zs[taps, pl.ds(place, 1), :]
            for i in range(7):
                total = total + zr[i, taps, pl.ds(place, 1), :]
            for k in range(TAPS):
                fs[row, group * TAPS + k : group * TAPS + k + 1, :] = total[k]
    final = [
        send(fs.at[0], fr.at[1], f_s.at[1], f_r.at[1], mirror_a),
        send(fs.at[1], fr.at[2], f_s.at[2], f_r.at[2], mirror_b),
        send(fs.at[1], fr.at[0], f_s.at[0], f_r.at[0], twin),
    ]

    total = jnp.zeros((1024, 256), F32)
    for k in range(K):
        total = total + dot(rk[k, :, 0:256], wb_own[k].reshape(256, 256), 1, 1)
    acc[...] = total

    for copy in d_gather:
        copy.wait_recv()

    def other_weight(k):
        return jnp.concatenate([wb_oth[k, b, a] for a in range(4) for b in range(4)], axis=0)

    total = acc[...]
    for k in range(K):
        total = total + dot(rk[k, :, 256:512], other_weight(k), 1, 1)
    acc[...] = total
    for seq in range(2):
        eo[:, 0:256] = acc[seq * 256 : seq * 256 + 256, :].astype(BF16)
        eo[:, 256:512] = acc[512 + seq * 256 : 768 + seq * 256, :].astype(BF16)
        gi[seq] = dot(eo[...], sv[...], 1, 0).astype(BF16)

    drain()
    for copy in final:
        copy.wait_recv()
    gw[:, 0, own_lanes] = fs[0, 0:K, :]
    gw[:, 0, oth_lanes] = fr[0, 0:K, :]
    value = fr[1:3].reshape(32, 256)
    high = value.astype(BF16)
    rest = value - high.astype(F32)
    mid = rest.astype(BF16)
    low = (rest - mid.astype(F32)).astype(BF16)
    reverse = dot(jnp.concatenate([high, mid, low], axis=0), flip, 1, 0)
    reverse = reverse[0:32] + reverse[32:64] + reverse[64:96]
    for half, lanes in enumerate((own_lanes, oth_lanes)):
        for k in range(K):
            gw[k, 1:2, lanes] = reverse[half * 16 + 8 - k : half * 16 + 9 - k]
    for side, at_end in enumerate((last_pos, first_pos)):

        @pl.when(jnp.logical_not(at_end))
        def _(side=side):
            edges[2 * side].wait_send()
            edges[2 * side + 1].wait_send()


def on_device(inputs, pre_act, grad_out, weight):
    sorts = jnp.asarray(channel_orders())
    dma = pltpu.SemaphoreType.DMA
    vmem = pltpu.VMEM
    grad_input, grad_weight = pl.pallas_call(
        kernel,
        out_shape=(vmem((2, 256, 512), BF16), vmem((K, 2, 512), F32)),
        in_specs=[pl.BlockSpec(memory_space=pl.ANY)] * 5,
        out_specs=[pl.BlockSpec(memory_space=vmem)] * 2,
        scratch_shapes=[
            vmem((K, 2, 512), BF16),
            vmem((2, 2, 256, 256), BF16),
            vmem((2, 2, 256, 256), BF16),
            vmem((2, 256, 512), BF16),
            vmem((512, 512), BF16),
            vmem((2, 256 + 2 * HALO, 512), F32),
            vmem((2, 256 + 2 * HALO, 512), F32),
            vmem((256, 1024), BF16),
            vmem((2, 256, 64), BF16),
            vmem((2, 16, 512), BF16),
            vmem((2, 16, 512), BF16),
            vmem((K, 1024, 512), BF16),
            vmem((2, 2 * HALO, 512), BF16),
            vmem((4, 2 * HALO, 512), BF16),
            vmem((4, 4, 2 * HALO, 256), F32),
            vmem((K, 64, 256), BF16),
            vmem((3, 16, 256), BF16),
            vmem((3, 16, 256), BF16),
            vmem((K, 16, 256), F32),
            vmem((K, 4, 4, 16, 256), BF16),
            vmem((K, 4, 4, 16, 256), BF16),
            vmem((K, 4, 4, 16, 256), F32),
            vmem((K, 4, 4, 16, 256), BF16),
            vmem((K, 4, 4, 16, 256), BF16),
            vmem((K, 4, 4, 16, 256), BF16),
            vmem((3, K, 4, 16, 256), BF16),
            vmem((K, 4, 16, 256), F32),
            vmem((K, 4, 16, 256), BF16),
            vmem((3, K, 16, 256), BF16),
            vmem((K, 16, 256), F32),
            vmem((7, K, 16, 256), F32),
            vmem((2, 16, 256), F32),
            vmem((3, 16, 256), F32),
            vmem((1024, 256), F32),
            vmem((256, 512), BF16),
            dma((7,)),
            dma((3,)), dma((3,)), dma((4,)), dma((4,)), dma((1,)), dma((1,)), dma((7,)), dma((7,)),
            dma((3,)), dma((3,)), dma((3,)), dma((3,)), dma((4,)), dma((4,)),
            dma((GROUPS,)), dma((GROUPS,)), dma((GROUPS, 3)), dma((GROUPS, 3)),
            dma((GROUPS, 3)), dma((GROUPS, 3)), dma((GROUPS, 7)), dma((GROUPS, 7)), dma((3,)), dma((3,)),
        ],
        compiler_params=pltpu.CompilerParams(
            collective_id=0, has_side_effects=True, vmem_limit_bytes=56 << 20
        ),
        name="conv_backward",
    )(jnp.transpose(weight, (1, 0, 2)), pre_act, grad_out, inputs, sorts)
    return grad_input, jnp.transpose(grad_weight, (1, 0, 2))


def solution(mesh):
    placed = (
        P("dp", "pos", None),
        P("dp", "pos", None),
        P("dp", "pos", None),
        P(("dp", "pos"), None, None),
    )
    return jax.shard_map(
        on_device,
        mesh=mesh,
        in_specs=placed,
        out_specs=(P("dp", "pos", None), P(("dp", "pos"), None, None)),
        check_vma=False,
    )
```

```python
import jax
import jax.numpy as jnp
import numpy as np
from jax import lax
from jax.experimental import pallas as pl
from jax.experimental.pallas import tpu as pltpu
from jax.sharding import PartitionSpec as P

K = 9
HALO = 8
GROUPS = 3
TAPS = K // GROUPS
MESH = pl.DeviceIdType.MESH
F32 = jnp.float32
BF16 = jnp.bfloat16


def gelu_slope(values):
    cdf = 0.5 * (1.0 + lax.erf(values * 0.7071067811865476))
    return cdf + values * jnp.exp(-0.5 * values * values) * 0.3989422804014327


def device(x, y, z, c):
    return ((y * 4 + z % 4) * 2 + c, (z // 4) * 4 + x)


def channel_orders():
    sorts = np.zeros((2, 512, 512), np.float32)
    for core in range(2):
        for q in range(4):
            for p in range(4):
                x, y = (p, q) if core == 0 else (q, p)
                for z in range(8):
                    for c in range(2):
                        row = (q * 4 + p) * 16 + 2 * z + c
                        dp, pos = device(x, y, z, c)
                        even = 2 * (dp * 8 + pos)
                        sorts[core, row, even] = 1.0
                        sorts[core, 256 + row, 511 - even] = 1.0
    return sorts.astype(jnp.bfloat16)


def dot(a, b, ca, cb):
    return lax.dot_general(a, b, (((ca,), (cb,)), ((), ())), preferred_element_type=F32)


def kernel(
    w_hbm, pre_hbm, go_hbm, x_hbm, sort_hbm, gi, gw,
    w_ref, pv, gv, xv, sv, gp, gfp, xt, xe, x_out, x_in, rk, edge_out, edge_in, edge_pad, edge_rows,
    mirror_out, mirror_in, zb, wb_own, wb_oth,
    sf, sd, dr, qs, qr, t1, ps, pr, zs, zr, fs, fr, acc, eo,
    load_sem, m_s, m_r, h_s, h_r, x_s, x_r, z_s, z_r, p_s, p_r, q_s, q_r, d_s, d_r,
    rd_s, rd_r, rq_s, rq_r, rp_s, rp_r, rz_s, rz_r, f_s, f_r,
):
    dp, pos = lax.axis_index("dp"), lax.axis_index("pos")
    y, c = dp // 8, dp % 2
    x = pos % 4
    z = (pos // 4) * 4 + (dp // 2) % 4
    p = x * (1 - c) + y * c
    q = y * (1 - c) + x * c
    z_steps = (4, 3, 5, 2, 6, 1, 7)
    z_peers = [device(x, y, (z + i) % 8, c) for i in z_steps]
    p_steps = (2, 1, 3)
    p_peers = [device((x + i * (1 - c)) % 4, (y + i * c) % 4, z, c) for i in p_steps]
    q_peers = [device((x + i * c) % 4, (y + i * (1 - c)) % 4, z, c) for i in p_steps]
    twin = device(x, y, z, 1 - c)
    mirror_a = device(3 - x, 3 - y, 7 - z, 1 - c)
    mirror_b = device(3 - x, 3 - y, 7 - z, c)
    other = dp + 1 - 2 * c
    beside = [(row, place) for place in ((pos + 1) % 8, (pos + 7) % 8) for row in (dp, other)]

    barrier = pltpu.get_barrier_semaphore()
    peers = [mirror_a, mirror_b] + beside + z_peers + p_peers + q_peers + [twin]
    for peer in peers:
        pl.semaphore_signal(barrier, inc=1, device_id=peer, device_id_type=MESH)

    own_lanes = pl.ds(pl.multiple_of(c * 256, 256), 256)
    oth_lanes = pl.ds(pl.multiple_of((1 - c) * 256, 256), 256)
    loads = [
        pltpu.make_async_copy(pre_hbm.at[:, :, own_lanes], pv.at[0], load_sem.at[0]),
        pltpu.make_async_copy(go_hbm.at[:, :, own_lanes], gv.at[0], load_sem.at[1]),
        pltpu.make_async_copy(pre_hbm.at[:, :, oth_lanes], pv.at[1], load_sem.at[2]),
        pltpu.make_async_copy(go_hbm.at[:, :, oth_lanes], gv.at[1], load_sem.at[3]),
        pltpu.make_async_copy(x_hbm, xv, load_sem.at[4]),
        pltpu.make_async_copy(sort_hbm.at[c], sv, load_sem.at[5]),
        pltpu.make_async_copy(w_hbm, w_ref, load_sem.at[6]),
    ]
    for load in loads:
        load.start()

    sends = []

    def drain():
        while sends:
            sends.pop(0).wait_send()


    def send(src, dst, send_sem, recv_sem, peer):
        copy = pltpu.make_async_remote_copy(
            src_ref=src, dst_ref=dst, send_sem=send_sem, recv_sem=recv_sem,
            device_id=peer, device_id_type=MESH,
        )
        copy.start()
        sends.append(copy)
        return copy

    rows_i = lax.broadcasted_iota(jnp.int32, (256, 256), 0)
    cols_i = lax.broadcasted_iota(jnp.int32, (256, 256), 1)
    flip = jnp.where(rows_i + cols_i == 255, 1.0, 0.0).astype(BF16)

    zeros = jnp.zeros((2, HALO, 512), F32)
    for padded in (gp, gfp):
        padded[:, 0:HALO, :] = zeros
        padded[:, HALO + 256 : 2 * HALO + 256, :] = zeros
    for half in range(2):
        loads[2 * half].wait()
        loads[2 * half + 1].wait()
        for seq in range(2):

            def slope(i, carry, half=half, seq=seq):
                rows = pl.ds(pl.multiple_of(i * 32, 32), 32)
                values = pv[half, seq, rows, :].astype(F32)
                grad = gv[half, seq, rows, :].astype(F32) * gelu_slope(values)
                place = pl.ds(pl.multiple_of(HALO + i * 32, 8), 32)
                gp[seq, place, half * 256 : half * 256 + 256] = grad.astype(BF16).astype(F32)
                return carry

            lax.fori_loop(0, 8, slope, 0)
    loads[6].wait()
    w_own = w_ref[:, :, own_lanes].astype(F32)
    w_oth = w_ref[:, :, oth_lanes].astype(F32)
    w0_own = w_own[:, 0, :]
    for i, row in enumerate((w_own[:, 1, :], w_oth[:, 1, :], w_oth[:, 0, :])):
        mirror_out[i] = jnp.concatenate([row, jnp.zeros((16 - K, 256), F32)], axis=0).astype(BF16)

    edge_out[0] = gp[:, 256 : 256 + HALO, :].reshape(2 * HALO, 512).astype(BF16)
    edge_out[1] = gp[:, HALO : 2 * HALO, :].reshape(2 * HALO, 512).astype(BF16)

    loads[4].wait()
    for end, start in enumerate((0, 248)):
        ends = [xv[seq, start : start + 8, :].astype(F32) for seq in range(2)]
        x_out[end] = jnp.concatenate(ends, axis=0).astype(BF16)

    pl.semaphore_wait(barrier, len(peers))
    edges = [
        pltpu.make_async_remote_copy(
            src_ref=edge_out.at[i // 2], dst_ref=edge_in.at[i],
            send_sem=h_s.at[i], recv_sem=h_r.at[i],
            device_id=peer, device_id_type=MESH,
        )
        for i, peer in enumerate(beside)
    ]
    last_pos, first_pos = pos == 7, pos == 0
    for side, at_end in enumerate((last_pos, first_pos)):

        @pl.when(jnp.logical_not(at_end))
        def _(side=side):
            edges[2 * side].start()
            edges[2 * side + 1].start()

    mirror = [
        send(mirror_out.at[i], mirror_in.at[i], m_s.at[i], m_r.at[i], peer)
        for i, peer in enumerate((mirror_a, mirror_b, twin))
    ]
    x_ends = send(x_out, x_in, x_s.at[0], x_r.at[0], twin)

    for seq in range(2):
        main = gp[seq, HALO : HALO + 256, :].astype(BF16)
        gfp[seq, HALO : HALO + 256, 0:256] = dot(main[:, 256:512], flip, 1, 0)
        gfp[seq, HALO : HALO + 256, 256:512] = dot(main[:, 0:256], flip, 1, 0)
    loads[5].wait()
    for seq in range(2):
        sorted_x = dot(sv[...], xv[seq], 1, 1).astype(BF16)
        xt[:, seq * 256 : seq * 256 + 256] = sorted_x[0:256]
        xt[:, 512 + seq * 256 : 768 + seq * 256] = sorted_x[256:512]
    for k in range(K):
        for seq in range(2):
            rk[k, seq * 256 : seq * 256 + 256, :] = gp[seq, 12 - k : 268 - k, :].astype(BF16)
            rk[k, 512 + seq * 256 : 768 + seq * 256, :] = gfp[seq, 4 + k : 260 + k, :].astype(BF16)

    def inner(k, carry):
        terms = dot(xt[...], rk[k], 1, 0)
        sf[k] = terms[:, 0:256].reshape(4, 4, 16, 256)
        for a in range(4):
            for b in range(4):
                rows = slice((a * 4 + b) * 16, (a * 4 + b) * 16 + 16)
                sd[k, b, a] = terms[rows, 256:512].astype(BF16)
        return carry

    twin_copies = []
    for group in range(GROUPS):
        lax.fori_loop(group * TAPS, group * TAPS + TAPS, inner, 0, unroll=True)
        taps = pl.ds(group * TAPS, TAPS)
        twin_copies.append(send(sd.at[taps], dr.at[taps], rd_s.at[group], rd_r.at[group], twin))

    x_ends.wait_recv()
    blank = jnp.zeros((32, 512), BF16)
    for i in range(2):
        even_rows = jnp.concatenate([x_out[1 - i], x_in[1 - i], blank], axis=0)
        odd_rows = jnp.concatenate([blank, x_out[i], x_in[i]], axis=0)
        xe[i] = (dot(sv[0:256, :], even_rows, 1, 1) + dot(sv[256:512, :], odd_rows, 1, 1)).astype(BF16)
    for copy in mirror:
        copy.wait_recv()
    rev_a = dot(mirror_in[0], flip, 1, 0)
    rev_b = dot(mirror_in[1], flip, 1, 0)
    w0_oth = mirror_in[2].astype(F32)
    for k in range(K):
        zb[k, pl.ds(2 * z + c, 1), :] = w0_own[k : k + 1] + rev_a[8 - k : 9 - k]
        zb[k, pl.ds(2 * z + 1 - c, 1), :] = w0_oth[k : k + 1] + rev_b[8 - k : 9 - k]
    mine = pl.ds(2 * z, 2)
    z_gather = [
        send(zb.at[:, mine, :], zb.at[:, mine, :], z_s.at[i], z_r.at[i], peer)
        for i, peer in enumerate(z_peers)
    ]

    for side, at_end in enumerate((first_pos, last_pos)):

        @pl.when(jnp.logical_not(at_end))
        def _(side=side):
            edges[2 * side].wait_recv()
            edges[2 * side + 1].wait_recv()

    border = [
        [jnp.where(at_end, 0.0, edge_in[2 * side + core].astype(F32)) for core in range(2)]
        for side, at_end in enumerate((first_pos, last_pos))
    ]
    low, high = [
        [
            border[side][core][seq * HALO : seq * HALO + HALO, core * 256 : core * 256 + 256]
            for core in range(2)
            for seq in range(2)
        ]
        for side in range(2)
    ]
    reverse_of = jnp.concatenate(
        [
            border[side][core][:, 256 - core * 256 : 512 - core * 256]
            for side in range(2)
            for core in range(2)
        ],
        axis=0,
    ).astype(BF16)
    reverse_of = dot(reverse_of, flip, 1, 0)
    blank = jnp.zeros((HALO, 256), F32)
    for seq in range(4):
        rev_low = reverse_of[seq * HALO : seq * HALO + HALO]
        rev_high = reverse_of[(4 + seq) * HALO : (5 + seq) * HALO]
        for i, parts in enumerate(
            ((blank, high[seq]), (rev_low, blank), (low[seq], blank), (blank, rev_high))
        ):
            edge_pad[i, seq, 0:HALO, :] = parts[0]
            edge_pad[i, seq, HALO : 2 * HALO, :] = parts[1]
    for k in range(K):
        first, second = (0, 1) if k <= 4 else (2, 3)
        start_1, start_2 = (4 - k, 4 + k) if k <= 4 else (12 - k, k - 4)
        rows_1 = [edge_pad[first, seq, start_1 : start_1 + 8, :] for seq in range(4)]
        rows_2 = [edge_pad[second, seq, start_2 : start_2 + 8, :] for seq in range(4)]
        edge_rows[k] = jnp.concatenate(rows_1 + rows_2, axis=0).astype(BF16)

    def chip_sum(group):
        twin_copies[group].wait_recv()

        def one(k, carry):
            terms = dot(xe[k // 5], edge_rows[k], 1, 0).reshape(4, 4, 16, 256)
            total = sf[k] + dr[k].astype(F32) + terms
            sf[k] = total
            qs[k] = total.astype(BF16)
            return carry

        lax.fori_loop(group * TAPS, group * TAPS + TAPS, one, 0, unroll=True)
        taps = pl.ds(group * TAPS, TAPS)
        return [
            send(
                qs.at[taps, (q + step) % 4], qr.at[i, taps],
                rq_s.at[group, i], rq_r.at[group, i], q_peers[i],
            )
            for i, step in enumerate(p_steps)
        ]

    def q_sum(group, copies):
        for copy in copies:
            copy.wait_recv()

        def one(k, carry):
            total = sf[k, q] + qr[0, k].astype(F32) + qr[1, k].astype(F32) + qr[2, k].astype(F32)
            t1[k] = total
            ps[k] = total.astype(BF16)
            return carry

        lax.fori_loop(group * TAPS, group * TAPS + TAPS, one, 0, unroll=True)
        taps = pl.ds(group * TAPS, TAPS)
        return [
            send(
                ps.at[taps, (p + step) % 4], pr.at[i, taps],
                rp_s.at[group, i], rp_r.at[group, i], p_peers[i],
            )
            for i, step in enumerate(p_steps)
        ]

    q_copies = [chip_sum(group) for group in range(GROUPS)]

    for copy in z_gather:
        copy.wait_recv()
    wb_own[:, q, p] = zb[...].astype(BF16)
    p_gather = [
        send(wb_own.at[:, q, p], wb_own.at[:, q, p], p_s.at[i], p_r.at[i], peer)
        for i, peer in enumerate(p_peers)
    ]
    low = jnp.where(first_pos, 0.0, edge_in[0].astype(F32)).reshape(2, HALO, 512)
    high = jnp.where(last_pos, 0.0, edge_in[2].astype(F32)).reshape(2, HALO, 512)
    gp[:, 0:HALO, :] = low
    gp[:, HALO + 256 : 2 * HALO + 256, :] = high
    both = jnp.concatenate([low[0], low[1], high[0], high[1]], axis=0).astype(BF16)
    both = jnp.concatenate(
        [dot(both[:, 256:512], flip, 1, 0), dot(both[:, 0:256], flip, 1, 0)], axis=1
    )
    for seq in range(2):
        gfp[seq, 0:HALO, :] = both[seq * HALO : seq * HALO + HALO]
        gfp[seq, HALO + 256 : 2 * HALO + 256, :] = both[(2 + seq) * HALO : (3 + seq) * HALO]
    for k in range(K):
        for seq in range(2):
            for start in (0, 240):
                rk[k, seq * 256 + start : seq * 256 + start + 16, :] = gp[
                    seq, 12 - k + start : 28 - k + start, :
                ].astype(BF16)
                rk[k, 512 + seq * 256 + start : 528 + seq * 256 + start, :] = gfp[
                    seq, 4 + k + start : 20 + k + start, :
                ].astype(BF16)

    p_copies = [q_sum(group, q_copies[group]) for group in range(GROUPS - 1)]
    for copy in p_gather:
        copy.wait_recv()
    q_gather = [
        send(wb_own.at[:, q], wb_own.at[:, q], q_s.at[i], q_r.at[i], peer)
        for i, peer in enumerate(q_peers)
    ]
    p_copies.append(q_sum(GROUPS - 1, q_copies[GROUPS - 1]))
    d_gather = [send(wb_own.at[:, q], wb_oth.at[:, q], d_s.at[0], d_r.at[0], twin)]
    def p_sum(k, carry):
        zs[k] = t1[k, p] + pr[0, k].astype(F32) + pr[1, k].astype(F32) + pr[2, k].astype(F32)
        return carry

    z_scatter = []
    for group in range(GROUPS):
        for copy in p_copies[group]:
            copy.wait_recv()
        lax.fori_loop(group * TAPS, group * TAPS + TAPS, p_sum, 0, unroll=True)
        taps = pl.ds(group * TAPS, TAPS)
        for i, step in enumerate(z_steps):
            rows = pl.ds(2 * ((z + step) % 8), 2)
            z_scatter.append(
                send(
                    zs.at[taps, rows, :], zr.at[i, taps, rows, :],
                    rz_s.at[group, i], rz_r.at[group, i], z_peers[i],
                )
            )

    for i in (1, 2, 0):
        q_gather[i].wait_recv()
        from_q = (q + 4 - p_steps[i]) % 4
        d_gather.append(
            send(wb_own.at[:, from_q], wb_oth.at[:, from_q], d_s.at[1 + i], d_r.at[1 + i], twin)
        )

    fs[:, 8:16, :] = jnp.zeros((2, 8, 256), F32)
    for group in range(GROUPS):
        for copy in z_scatter[group * 7 : group * 7 + 7]:
            copy.wait_recv()
        taps = slice(group * TAPS, group * TAPS + TAPS)
        for row, place in enumerate((2 * z + c, 2 * z + 1 - c)):
            total = zs[taps, pl.ds(place, 1), :]
            for i in range(7):
                total = total + zr[i, taps, pl.ds(place, 1), :]
            for k in range(TAPS):
                fs[row, group * TAPS + k : group * TAPS + k + 1, :] = total[k]
    final = [
        send(fs.at[0], fr.at[1], f_s.at[1], f_r.at[1], mirror_a),
        send(fs.at[1], fr.at[2], f_s.at[2], f_r.at[2], mirror_b),
        send(fs.at[1], fr.at[0], f_s.at[0], f_r.at[0], twin),
    ]

    total = jnp.zeros((1024, 256), F32)
    for k in range(K):
        total = total + dot(rk[k, :, 0:256], wb_own[k].reshape(256, 256), 1, 1)
    acc[...] = total

    for copy in d_gather:
        copy.wait_recv()

    def other_weight(k):
        return jnp.concatenate([wb_oth[k, b, a] for a in range(4) for b in range(4)], axis=0)

    total = acc[...]
    for k in range(K):
        total = total + dot(rk[k, :, 256:512], other_weight(k), 1, 1)
    acc[...] = total
    for seq in range(2):
        eo[:, 0:256] = acc[seq * 256 : seq * 256 + 256, :].astype(BF16)
        eo[:, 256:512] = acc[512 + seq * 256 : 768 + seq * 256, :].astype(BF16)
        gi[seq] = dot(eo[...], sv[...], 1, 0).astype(BF16)

    drain()
    for copy in final:
        copy.wait_recv()
    gw[:, 0, own_lanes] = fs[0, 0:K, :]
    gw[:, 0, oth_lanes] = fr[0, 0:K, :]
    value = fr[1:3].reshape(32, 256)
    high = value.astype(BF16)
    rest = value - high.astype(F32)
    mid = rest.astype(BF16)
    low = (rest - mid.astype(F32)).astype(BF16)
    reverse = dot(jnp.concatenate([high, mid, low], axis=0), flip, 1, 0)
    reverse = reverse[0:32] + reverse[32:64] + reverse[64:96]
    for half, lanes in enumerate((own_lanes, oth_lanes)):
        for k in range(K):
            gw[k, 1:2, lanes] = reverse[half * 16 + 8 - k : half * 16 + 9 - k]
    for side, at_end in enumerate((last_pos, first_pos)):

        @pl.when(jnp.logical_not(at_end))
        def _(side=side):
            edges[2 * side].wait_send()
            edges[2 * side + 1].wait_send()


def on_device(inputs, pre_act, grad_out, weight):
    sorts = jnp.asarray(channel_orders())
    dma = pltpu.SemaphoreType.DMA
    vmem = pltpu.VMEM
    grad_input, grad_weight = pl.pallas_call(
        kernel,
        out_shape=(vmem((2, 256, 512), BF16), vmem((K, 2, 512), F32)),
        in_specs=[pl.BlockSpec(memory_space=pl.ANY)] * 5,
        out_specs=[pl.BlockSpec(memory_space=vmem)] * 2,
        scratch_shapes=[
            vmem((K, 2, 512), BF16),
            vmem((2, 2, 256, 256), BF16),
            vmem((2, 2, 256, 256), BF16),
            vmem((2, 256, 512), BF16),
            vmem((512, 512), BF16),
            vmem((2, 256 + 2 * HALO, 512), F32),
            vmem((2, 256 + 2 * HALO, 512), F32),
            vmem((256, 1024), BF16),
            vmem((2, 256, 64), BF16),
            vmem((2, 16, 512), BF16),
            vmem((2, 16, 512), BF16),
            vmem((K, 1024, 512), BF16),
            vmem((2, 2 * HALO, 512), BF16),
            vmem((4, 2 * HALO, 512), BF16),
            vmem((4, 4, 2 * HALO, 256), F32),
            vmem((K, 64, 256), BF16),
            vmem((3, 16, 256), BF16),
            vmem((3, 16, 256), BF16),
            vmem((K, 16, 256), F32),
            vmem((K, 4, 4, 16, 256), BF16),
            vmem((K, 4, 4, 16, 256), BF16),
            vmem((K, 4, 4, 16, 256), F32),
            vmem((K, 4, 4, 16, 256), BF16),
            vmem((K, 4, 4, 16, 256), BF16),
            vmem((K, 4, 4, 16, 256), BF16),
            vmem((3, K, 4, 16, 256), BF16),
            vmem((K, 4, 16, 256), F32),
            vmem((K, 4, 16, 256), BF16),
            vmem((3, K, 16, 256), BF16),
            vmem((K, 16, 256), F32),
            vmem((7, K, 16, 256), F32),
            vmem((2, 16, 256), F32),
            vmem((3, 16, 256), F32),
            vmem((1024, 256), F32),
            vmem((256, 512), BF16),
            dma((7,)),
            dma((3,)), dma((3,)), dma((4,)), dma((4,)), dma((1,)), dma((1,)), dma((7,)), dma((7,)),
            dma((3,)), dma((3,)), dma((3,)), dma((3,)), dma((4,)), dma((4,)),
            dma((GROUPS,)), dma((GROUPS,)), dma((GROUPS, 3)), dma((GROUPS, 3)),
            dma((GROUPS, 3)), dma((GROUPS, 3)), dma((GROUPS, 7)), dma((GROUPS, 7)), dma((3,)), dma((3,)),
        ],
        compiler_params=pltpu.CompilerParams(
            collective_id=0, has_side_effects=True, vmem_limit_bytes=56 << 20
        ),
        name="conv_backward",
    )(jnp.transpose(weight, (1, 0, 2)), pre_act, grad_out, inputs, sorts)
    return grad_input, jnp.transpose(grad_weight, (1, 0, 2))


def solution(mesh):
    placed = (
        P("dp", "pos", None),
        P("dp", "pos", None),
        P("dp", "pos", None),
        P(("dp", "pos"), None, None),
    )
    return jax.shard_map(
        on_device,
        mesh=mesh,
        in_specs=placed,
        out_specs=(P("dp", "pos", None), P(("dp", "pos"), None, None)),
        check_vma=False,
    )
```
